32 devices in a mesh: gz: 2 (over y), gy: 4 (over x, core), gx: 4 (over z).
Axes of the slice: x: 2, y: 2, z: 4, core: 2. Of those that a mesh axis runs over, the one named last changes fastest.
Arguments:
- labels: int32 [2, 32, 512], P('gz', 'gy', 'gx'), may hold values from 0 to 7
- tissue_tensors: float32 [6, 8], replicated, as said below
- electrodes: int32 [2, 64], replicated, may hold values from 0 to 32767, as said below
- initial: float32 [64, 2, 32, 512], P(None, 'gz', 'gy', 'gx'), may hold values from -4 to 4
Outputs:
- solution: float32 [64, 2, 32, 512], P(None, 'gz', 'gy', 'gx')
- residual: float32 [64, 2, 32, 512], P(None, 'gz', 'gy', 'gx')
The draws below stay inside these ranges and needn't reach their ends.
Inputs may be any that keep to these rules, and one draw needn't show every extreme that they name: `tissue_tensors`: the tensors are symmetric and positive definite: each off-diagonal component is at most 0.3 times the geometric mean of its two diagonal components. `electrodes`: all 128 voxel indices are distinct; voxel (z, y, x) has index (z * 32 + y) * 512 + x.
All inputs are finite; a program needn't handle non-finite values.
Results may differ from the reference program's by a relative error of at most 0.0003.
Values sent between devices are 32-bit elements; how exact they have to be, the bound alone decides.
A program may use at most 64 MiB of HBM per device.

```python
import math
import jax
import jax.numpy as jnp
from jax import lax

LEADS = 64
TISSUES = 8
ITERS = 2
NZ = 2
NY = 32
NX = 512


def draw_tissue_tensors(key, part):
    first_key, second_key = jax.random.split(key)
    diagonal = jnp.exp(jax.random.uniform(first_key, (3, TISSUES), jnp.float32, jnp.log(0.2), jnp.log(2.0)))
    spread = jax.random.uniform(second_key, (3, TISSUES), jnp.float32, -1.0, 1.0)
    coupling_xy = 0.3 * spread[0] * jnp.sqrt(diagonal[0] * diagonal[1])
    coupling_xz = 0.3 * spread[1] * jnp.sqrt(diagonal[0] * diagonal[2])
    coupling_yz = 0.3 * spread[2] * jnp.sqrt(diagonal[1] * diagonal[2])
    return jnp.concatenate([diagonal, jnp.stack([coupling_xy, coupling_xz, coupling_yz])], axis=0).astype(jnp.float32)


def draw_electrodes(key, part):
    first_key, second_key = jax.random.split(key)
    count_all = 2 * LEADS
    stratum = NZ * NY * NX // count_all
    offsets = jax.random.randint(first_key, (count_all,), 0, stratum, jnp.int32)
    shuffle = jax.random.permutation(second_key, jnp.arange(count_all, dtype=jnp.int32))
    return (shuffle * stratum + offsets).reshape(2, LEADS).astype(jnp.int32)


def draw_initial(key, part):
    phase_key, freq_key, noise_key = jax.random.split(jax.random.fold_in(key, 7), 3)
    shape = (LEADS, NZ, NY, NX)
    phases = jax.random.uniform(phase_key, (3, LEADS), jnp.float32, -math.pi, math.pi)
    freqs = jax.random.uniform(freq_key, (3, LEADS), jnp.float32, 0.5, 2.0)
    depth = (lax.broadcasted_iota(jnp.float32, (1, NZ, 1, 1), 1) + 0.5) / NZ
    rows = (lax.broadcasted_iota(jnp.float32, (1, 1, NY, 1), 2) + 0.5) / NY
    cols = (lax.broadcasted_iota(jnp.float32, (1, 1, 1, NX), 3) + 0.5) / NX

    def wave(index, coord):
        return 2.0 * math.pi * freqs[index][:, None, None, None] * coord + phases[index][:, None, None, None]
    smooth = jnp.sin(wave(0, depth)) * jnp.cos(wave(1, rows)) + jnp.sin(wave(2, cols))
    noise = jnp.clip(jax.random.normal(noise_key, shape, jnp.float32), -4.0, 4.0)
    value = smooth + 0.5 * noise
    return value.astype(jnp.float32)


def with_ends(array, rng, smallest, top_value):
    longest = array.shape.index(max(array.shape))
    spots = []
    for shift in (0, 1):
        where = [jax.random.randint(jax.random.fold_in(rng, axis), (), 0, length) for axis, length in enumerate(array.shape)]
        where[longest] = (where[longest] + shift) % array.shape[longest]
        spots.append(tuple(where))
    return array.at[spots[0]].set(smallest).at[spots[1]].set(top_value)


def setup_inputs(seed: int = 0) -> dict:
    splits = jax.random.split(jax.random.key(seed), 5)
    return {
        "labels": with_ends(jax.random.randint(splits[0], (NZ, NY, NX), 0, TISSUES), jax.random.fold_in(splits[0], 1), 0, TISSUES - 1).astype(jnp.int32),
        "tissue_tensors": draw_tissue_tensors(jax.random.fold_in(splits[4], 71), 0),
        "electrodes": draw_electrodes(jax.random.fold_in(splits[4], 71), 0),
        "initial": draw_initial(jax.random.fold_in(splits[4], 71), 0),
    }


def tensor_lookup(labels, table):
    result = jnp.zeros((6,) + labels.shape, jnp.float32)
    for tissue in range(table.shape[1]):
        result = result + jnp.where(labels[None] == tissue, table[:, tissue][:, None, None, None], jnp.float32(0.0))
    return result

def flux_terms(tensor, grad_x, grad_y, grad_z):
    flux_x = tensor[0] * grad_x + tensor[3] * grad_y + tensor[4] * grad_z
    flux_y = tensor[3] * grad_x + tensor[1] * grad_y + tensor[5] * grad_z
    flux_z = tensor[4] * grad_x + tensor[5] * grad_y + tensor[2] * grad_z
    return (flux_x, flux_y, flux_z)

def operate_block(group, tensor_padded):
    padded = jnp.pad(group, ((0, 0), (1, 1), (1, 1), (1, 1)))
    centre = padded[:, :-1, :-1, :-1]
    grad_z = padded[:, 1:, :-1, :-1] - centre
    grad_y = padded[:, :-1, 1:, :-1] - centre
    grad_x = padded[:, :-1, :-1, 1:] - centre
    tensor_box = tensor_padded[:, :-1, :-1, :-1]
    flux_x, flux_y, flux_z = flux_terms(tensor_box, grad_x, grad_y, grad_z)
    return flux_z[:, :-1, 1:, 1:] - flux_z[:, 1:, 1:, 1:] + (flux_y[:, 1:, :-1, 1:] - flux_y[:, 1:, 1:, 1:]) + (flux_x[:, 1:, 1:, :-1] - flux_x[:, 1:, 1:, 1:])

def gram_of(first, second):
    leads = first.shape[0]
    return lax.dot_general(first.reshape(leads, -1).astype(jnp.float32), second.reshape(leads, -1).astype(jnp.float32), (((1,), (1,)), ((), ())), precision=lax.Precision.HIGHEST, preferred_element_type=jnp.float32)

def combine_rows(coef, field):
    leads = field.shape[0]
    return jnp.dot(coef.T.astype(jnp.float32), field.reshape(leads, -1).astype(jnp.float32), precision=lax.Precision.HIGHEST, preferred_element_type=jnp.float32).reshape(field.shape)

def factor_solve(matrix, target):
    factor = jnp.linalg.cholesky(matrix)
    halfway = lax.linalg.triangular_solve(factor, target, left_side=True, lower=True)
    return lax.linalg.triangular_solve(factor, halfway, left_side=True, lower=True, transpose_a=True)

def reference(labels, tissue_tensors, electrodes, initial):
    shape = labels.shape
    depth_ids = lax.broadcasted_iota(jnp.int32, shape, 0)
    row_ids = lax.broadcasted_iota(jnp.int32, shape, 1)
    col_ids = lax.broadcasted_iota(jnp.int32, shape, 2)
    voxel_id = (depth_ids * NY + row_ids) * NX + col_ids
    sources = (voxel_id[None] == electrodes[0][:, None, None, None]).astype(jnp.float32) - (voxel_id[None] == electrodes[1][:, None, None, None]).astype(jnp.float32)
    tensor = tensor_lookup(labels, tissue_tensors)
    tensor_padded = jnp.pad(tensor, ((0, 0), (1, 1), (1, 1), (1, 1)))

    def operate(field):
        groups = field.reshape((LEADS // 8, 8) + shape)
        return lax.map(lambda group: operate_block(group, tensor_padded), groups).reshape(field.shape)
    solution = initial
    residual = sources - operate(initial)
    direction = residual
    rr_now = gram_of(residual, residual)
    for iteration in range(ITERS):
        image = operate(direction)
        curve = gram_of(direction, image)
        step_coef = factor_solve(curve, rr_now)
        solution = solution + combine_rows(step_coef, direction)
        residual = residual - combine_rows(step_coef, image)
        if iteration + 1 < ITERS:
            rr_next = gram_of(residual, residual)
            beta_coef = factor_solve(rr_now, rr_next)
            direction = residual + combine_rows(beta_coef, direction)
            rr_now = rr_next
    return (solution, residual)
```

```python
import jax
import jax.numpy as jnp
from jax import lax
from jax.experimental import pallas as pl
from jax.experimental.pallas import tpu as pltpu
from jax.sharding import PartitionSpec as P

MESH = pl.DeviceIdType.MESH
HIGH = lax.Precision.HIGHEST
DEPTH = 3
VMEM_LIMIT = 58 * 1024 * 1024


def nt_dot(a, b):
    return lax.dot_general(
        a, b, (((1,), (1,)), ((), ())), precision=HIGH, preferred_element_type=jnp.float32
    )


def nn_dot(a, b):
    return lax.dot_general(
        a, b, (((1,), (0,)), ((), ())), precision=HIGH, preferred_element_type=jnp.float32
    )


def make_krylov(nz, ny, nx, leads, rows, cols, classes):
    windowed = nz > DEPTH + 1
    layers = 2 * DEPTH + 1 if windowed else nz
    ext = rows + 2 * DEPTH
    top = DEPTH + rows
    if windowed:
        offsets = [d for d in range(-DEPTH, DEPTH + 1) if d]
    else:
        offsets = list(range(1, nz))
    noff = len(offsets)
    groups = leads // 8
    per = 2
    nch = groups // per
    span = per * 8
    plane = nz * ny
    size = 2 * leads
    flat = plane * nx <= 64
    owners = plane * nx if flat else plane
    share = size // owners
    last = cols - 1

    def kernel(
        table_hbm, labels_hbm, electrodes_hbm, field_hbm, base_hbm, gram_hbm,
        base_out, total, ssem, table, labels, electrodes, field, lsem,
        xe, lt, lab, lp, lr, xs, xr, re, qe, pe, coef, inside, hcoef, hinside, elec, gs, rs, zs,
        zsend, zrecv, ysend, yrecv, xsend, xrecv, asend, arecv,
    ):
        z, y, x = lax.axis_index("gz"), lax.axis_index("gy"), lax.axis_index("gx")
        own = DEPTH if windowed else z
        first = z - DEPTH if windowed else 0
        zs_ = [lax.rem(z + d, nz) for d in range(nz)]
        ys_ = [lax.rem(y + d, ny) for d in range(ny)]
        xs_ = [lax.rem(x + d, nx) for d in range(nx)]
        plane_peers = [
            (zs_[dz] * ny + ys_[dy], {"gz": zs_[dz], "gy": ys_[dy]})
            for dz in range(nz)
            for dy in range(ny)
        ]
        line_peers = [(xs_[dx], {"gx": xs_[dx]}) for dx in range(nx)]
        if flat:
            all_peers = [
                (pid * nx + xid, {**pdev, **xdev})
                for pid, pdev in plane_peers
                for xid, xdev in line_peers
            ]
            greeted = all_peers[1:]
        else:
            greeted = plane_peers[1:] + line_peers[1:]

        loads = [
            pltpu.make_async_copy(source, target, lsem.at[i])
            for i, (source, target) in enumerate(
                (
                    (field_hbm, field), (labels_hbm, labels),
                    (electrodes_hbm, electrodes), (table_hbm, table),
                )
            )
        ]
        for load in loads:
            load.start()
        barrier = pltpu.get_barrier_semaphore()
        for _, device in greeted:
            pl.semaphore_signal(barrier, inc=1, device_id=device, device_id_type=MESH)

        outside = jnp.full((8, cols), -1.0, jnp.float32)

        def fill(slot, lo, hi):
            for r in range(lo, hi):
                xe[slot, r] = jnp.zeros((leads, cols), jnp.float32)

        if windowed:
            for s in range(layers):

                @pl.when((first + s < 0) | (first + s >= nz))
                def _(s=s):
                    fill(s, 0, ext)
                    for j in range(3):
                        lt[s, j] = outside

        for s in range(layers):

            @pl.when(y == 0)
            def _(s=s):
                fill(s, 0, DEPTH)
                lt[s, 1] = outside

            @pl.when(y == ny - 1)
            def _(s=s):
                fill(s, top, ext)
                lt[s, 2] = outside

        for side, edge in ((0, nx - 1), (1, 0)):

            @pl.when(x == edge)
            def _(side=side):
                for s in range(layers):
                    xr[side, s] = jnp.zeros((leads, cols), jnp.float32)
                    lr[side, s] = outside

        for load in loads:
            load.wait()
        lt[own, 0] = labels[...].astype(jnp.float32)
        for r in range(rows):
            xe[own, DEPTH + r] = field[pl.ds(r, leads, stride=rows), :]
        pl.semaphore_wait(barrier, len(greeted))

        def z_plan(i):
            d = offsets[i]
            if windowed:
                return (
                    z + d, DEPTH - d, DEPTH - d,
                    (z + d >= 0) & (z + d < nz), (z - d >= 0) & (z - d < nz),
                )
            return lax.rem(z + d, nz), z, lax.rem(z - d + nz, nz), None, None

        def when(cond, action):
            if cond is None:
                action()
            else:
                pl.when(cond)(action)

        def remote(src, dst, send, recv, device):
            return pltpu.make_async_remote_copy(
                src_ref=src, dst_ref=dst, send_sem=send, recv_sem=recv,
                device_id=device, device_id_type=MESH,
            )

        def chunk(c):
            if c is None:
                return slice(0, leads)
            if isinstance(c, int):
                return slice(c * span, (c + 1) * span)
            return pl.ds(pl.multiple_of(c * span, 8), span)

        def z_copies(i, c):
            peer, slot, _, _, _ = z_plan(i)
            device = {"gz": peer}
            body = remote(
                xe.at[own, DEPTH:top, chunk(c), :], xe.at[slot, DEPTH:top, chunk(c), :],
                zsend.at[i, c], zrecv.at[i, c], device,
            )
            if c != 0:
                return [body]
            return [
                remote(lt.at[own, 0], lt.at[slot, 0], zsend.at[i, nch], zrecv.at[i, nch], device),
                body,
            ]

        def y_copies(i, slot, up, c, tile):
            src = (top - DEPTH, top) if up else (DEPTH, 2 * DEPTH)
            dst = (0, DEPTH) if up else (top, ext)
            device = {"gy": y + 1 if up else y - 1}
            at = 0 if c is None else c
            copies = [
                remote(
                    xe.at[slot, src[0] : src[1], chunk(c), :],
                    xe.at[slot, dst[0] : dst[1], chunk(c), :],
                    ysend.at[i, up, at], yrecv.at[i, up, at], device,
                )
            ]
            if tile:
                copies.insert(
                    0,
                    remote(
                        lt.at[slot, 0], lt.at[slot, 1 if up else 2],
                        ysend.at[i, up, nch], yrecv.at[i, up, nch], device,
                    ),
                )
            return copies

        def x_copies(i, slot, side, c, tile):
            device = {"gx": x + 1 if side else x - 1}
            at = 0 if c is None else c
            copies = [
                remote(
                    xs.at[slot, chunk(c), :], xr.at[side, slot, chunk(c), :],
                    xsend.at[i, side, at], xrecv.at[i, side, at], device,
                )
            ]
            if tile:
                copies.insert(
                    0,
                    remote(
                        lp.at[slot], lr.at[side, slot],
                        xsend.at[i, side, nch], xrecv.at[i, side, nch], device,
                    ),
                )
            return copies

        has_low, has_high = y > 0, y < ny - 1
        ysends = (has_low, has_high)
        xsends = (x > 0, x < nx - 1)

        def start(copies):
            for copy in copies:
                copy.start()

        def wait_send(copies):
            for copy in copies:
                copy.wait_send()

        def wait_recv(copies):
            for copy in copies:
                copy.wait_recv()

        def both(sends, make, action, mirrored=False):
            for side in (1, 0):
                pl.when(sends[1 - side if mirrored else side])(
                    lambda side=side: action(make(side))
                )

        for c in range(nch):
            for i in range(noff):
                when(z_plan(i)[3], lambda i=i, c=c: start(z_copies(i, c)))
            if c == 0:
                both(ysends, lambda up: y_copies(noff, own, up, None, True), start)

        eye = lax.broadcasted_iota(jnp.int32, (leads, leads), 0) == lax.broadcasted_iota(
            jnp.int32, (leads, leads), 1
        )
        for e in range(2):
            line = electrodes[e : e + 1, :].astype(jnp.float32)
            column = jnp.sum(
                jnp.where(eye, jnp.broadcast_to(line, (leads, leads)), 0.0), axis=1, keepdims=True
            )
            elec[e] = jnp.broadcast_to(column, (leads, cols))

        def group(c):
            return pl.ds(pl.multiple_of(c * 8, 8), 8)

        lane = lax.broadcasted_iota(jnp.int32, (8, cols), 1)

        def gather_edges(load):
            total = jnp.zeros((8, cols), jnp.float32)
            for r in range(ext):
                moved = pltpu.roll(load(r), 8 * r, axis=1) if r else load(r)
                if r == 0:
                    keep = (lane < DEPTH) | (lane >= cols - DEPTH)
                else:
                    keep = (lane >= 8 * r - DEPTH) & (lane < 8 * r + DEPTH)
                total = jnp.where(keep, moved, total)
            return total

        def pack(slot, lo, hi):
            def step(c, _):
                xs[slot, group(c), :] = gather_edges(lambda r: xe[slot, r, group(c), :])
                return 0

            lax.fori_loop(lo, hi, step, 0)

        def pack_labels(slot):
            for r in range(ext):
                if r < DEPTH:
                    row = lt[slot, 1, rows - DEPTH + r : rows - DEPTH + r + 1, :]
                elif r < top:
                    row = lt[slot, 0, r - DEPTH : r - DEPTH + 1, :]
                else:
                    row = lt[slot, 2, r - top : r - top + 1, :]
                lab[slot, r] = jnp.broadcast_to(row, (8, cols))
            lp[slot] = gather_edges(lambda r: lab[slot, r])

        def forward_y(c):
            for i in range(noff):

                def arrived(i=i):
                    wait_recv(z_copies(i, c))
                    slot = z_plan(i)[2]
                    both(ysends, lambda up: y_copies(i, slot, up, c, c == 0), start)

                when(z_plan(i)[4], arrived)

        def forward_x(c):
            tile = isinstance(c, int) and c == 0
            for i in range(noff):
                slot = z_plan(i)[2]

                def arrived(i=i, slot=slot):
                    make = lambda up: y_copies(i, slot, up, c, tile)
                    both(ysends, make, wait_recv, mirrored=True)

                when(z_plan(i)[4], arrived)
                if tile:
                    pack_labels(slot)
                pack(slot, c * per, (c + 1) * per)
                both(xsends, lambda side: x_copies(i, slot, side, c, tile), start)

        both(ysends, lambda up: y_copies(noff, own, up, None, True), wait_recv, mirrored=True)
        pack_labels(own)
        pack(own, 0, groups)
        both(xsends, lambda side: x_copies(noff, own, side, None, True), start)

        forward_y(0)
        for c in range(1, nch):
            forward_y(c)
            if c <= nch - 2:
                forward_x(c - 1)

        both(xsends, lambda side: x_copies(noff, own, side, None, True), wait_recv, mirrored=True)
        for i in range(noff):
            slot = z_plan(i)[2]
            both(
                xsends, lambda side: x_copies(i, slot, side, 0, True)[:1], wait_recv, mirrored=True
            )

        values = [[table[i, t] for t in range(table.shape[1])] for i in range(6)]

        def look(label):
            parts = [jnp.zeros(label.shape, jnp.float32)] * 6
            for t in range(table.shape[1]):
                match = label == float(t)
                parts = [jnp.where(match, values[i][t], parts[i]) for i in range(6)]
            return parts, jnp.where(label >= 0.0, 1.0, 0.0)

        near = (lane & 7) < 4

        def lookup(r, _):
            for s in range(layers):
                parts, here = look(lab[s, r])
                for i in range(6):
                    coef[i, s, r] = parts[i]
                inside[s, r] = here
            return 0

        lax.fori_loop(0, ext, lookup, 0)
        for s in range(layers):
            for side in (0, 1):
                label = (
                    jnp.where(near, lp[s], lr[1, s]) if side else jnp.where(near, lr[0, s], lp[s])
                )
                parts, here = look(label)
                for i in range(6):
                    hcoef[i, s, side] = parts[i]
                hinside[s, side] = here

        line_width = nx * cols
        column = (x * cols + lane).astype(jnp.float32)
        moved = jnp.where(lane >= cols - DEPTH, lane + DEPTH - cols, lane + DEPTH)
        packed_row = moved // 8
        packed_voxel = packed_row * line_width + (moved - packed_row * 8) + (
            x * cols + (y * rows - DEPTH) * line_width - DEPTH
        )
        ends = (lane == 0, lane == last)
        seam = (lane & 7) == 7

        def source(c, voxel):
            return jnp.where(
                elec[0, group(c), :] == voxel, 1.0,
                jnp.where(elec[1, group(c), :] == voxel, -1.0, 0.0),
            )

        def flux(t, axis, grads):
            order = ((0, 3, 4), (3, 1, 5), (4, 5, 2))[axis]
            return t[order[0]] * grads[0] + t[order[1]] * grads[1] + t[order[2]] * grads[2]

        def rim(fields, side, full):
            sums, edges = [], []
            below = None
            for s in range(layers):
                t = [hcoef[i, s, side] for i in range(6)]
                v = fields[s]
                grads = (
                    pltpu.roll(v, last, axis=1) - v,
                    pltpu.roll(v, cols - 8, axis=1) - v,
                    fields[s + 1] - v if s + 1 < layers else -v,
                )
                flux_x = flux(t, 0, grads)
                edges.append(flux_x)
                if full:
                    flux_y, flux_z = flux(t, 1, grads), flux(t, 2, grads)
                    total = (pltpu.roll(flux_y, 8, axis=1) - flux_y) + (
                        pltpu.roll(flux_x, 1, axis=1) - flux_x
                    )
                    total = total - flux_z if below is None else total + (below - flux_z)
                    below = flux_z
                    sums.append(total)
            return sums, edges

        def seams(right, edges):
            return [
                jnp.where(seam, edges[s], pltpu.roll(right[s], cols - 2, axis=1))
                for s in range(layers)
            ]

        def operate(load, emit, lo, hi, joins):
            below_y = [None] * layers
            for r in range(lo - 1, hi):
                here = [load(s, r) for s in range(layers)]
                below_z = None
                for s in range(layers):
                    t = [coef[i, s, r] for i in range(6)]
                    v = here[s]
                    join = pltpu.roll(joins[s], (cols + 1 - 8 * r) % cols, axis=1)
                    grads = (
                        jnp.where(ends[1], join, pltpu.roll(v, last, axis=1)) - v,
                        load(s, r + 1) - v,
                        here[s + 1] - v if s + 1 < layers else -v,
                    )
                    flux_y = flux(t, 1, grads)
                    if r >= lo:
                        flux_x, flux_z = flux(t, 0, grads), flux(t, 2, grads)
                        before = jnp.where(ends[0], join, pltpu.roll(flux_x, 1, axis=1))
                        total = (below_y[s] - flux_y) + (before - flux_x)
                        total = total - flux_z if below_z is None else total + (below_z - flux_z)
                        emit(s, r, total)
                        below_z = flux_z
                    below_y[s] = flux_y

        def advance(c):
            mine = [xs[s, group(c), :] for s in range(layers)]
            right = [jnp.where(near, xr[0, s, group(c), :], mine[s]) for s in range(layers)]
            left = [jnp.where(near, mine[s], xr[1, s, group(c), :]) for s in range(layers)]
            right_sum, _ = rim(right, 0, True)
            left_sum, left_edge = rim(left, 1, True)
            joins_v = seams(right, left_edge)
            plane_voxels = ny * rows * line_width

            def rim_r(total, s, side):
                voxel = packed_voxel + ((first + s) * plane_voxels + (0 if side else cols))
                return (source(c, voxel.astype(jnp.float32)) - total) * hinside[s, side]

            right_r = [rim_r(right_sum[s], s, 0) for s in range(layers)]
            left_r = [rim_r(left_sum[s], s, 1) for s in range(layers)]
            right_sum, _ = rim(right_r, 0, True)
            left_sum, left_edge = rim(left_r, 1, True)
            joins_r = seams(right_r, left_edge)
            right_q = [right_sum[s] * hinside[s, 0] for s in range(layers)]
            left_q = [left_sum[s] * hinside[s, 1] for s in range(layers)]
            _, left_edge = rim(left_q, 1, False)
            joins_q = seams(right_q, left_edge)

            def emit_r(s, r, total):
                row = (first + s) * (ny * rows) + y * rows + (r - DEPTH)
                voxel = column + (row * line_width).astype(jnp.float32)
                re[s, r] = (source(c, voxel) - total) * inside[s, r]

            def emit_q(s, r, total):
                qe[s, r] = total * inside[s, r]

            def emit_p(s, r, total):
                pe[s, r - DEPTH] = total

            operate(lambda s, r: xe[s, r, group(c), :], emit_r, 1, ext - 1, joins_v)
            operate(lambda s, r: re[s, r], emit_q, 2, ext - 2, joins_r)
            operate(lambda s, r: qe[s, r], emit_p, 3, ext - 3, joins_q)
            for r in range(rows):
                at = slice(r * cols, (r + 1) * cols)
                base_out[group(c), at] = re[own, DEPTH + r]
                base_out[group(c + groups), at] = qe[own, DEPTH + r]
                base_out[group(c + 2 * groups), at] = pe[own, r]

        def turn(c, _):
            @pl.when(c < 2)
            def _():
                forward_x(c + (nch - 2))

            for i in range(noff):
                slot = z_plan(i)[2]
                both(
                    xsends, lambda side: x_copies(i, slot, side, c, False), wait_recv,
                    mirrored=True,
                )

            def step(g, _):
                advance(c * per + g)
                return 0

            lax.fori_loop(0, per, step, 0)
            return 0

        lax.fori_loop(0, nch, turn, 0)

        upper = nt_dot(base_out[0:leads, :], base_out[0 : 2 * leads, :])
        lower = nt_dot(base_out[leads : 2 * leads, :], base_out[leads : 3 * leads, :])
        grams = jnp.concatenate([upper, lower], axis=0)
        for i in range(owners):
            gs[i] = grams[i * share : (i + 1) * share, :]

        save = pltpu.make_async_copy(base_out, base_hbm, ssem.at[0])
        save.start()

        def exchange(phase, peers, source_of, target):
            copies = [
                remote(source_of(pid), target, asend.at[phase, k], arecv.at[phase, k], device)
                for k, (pid, device) in enumerate(peers)
                if k
            ]
            start(copies)
            for copy in copies:
                copy.wait()

        peers = all_peers if flat else plane_peers
        me = peers[0][0]
        rs[me] = gs[me]
        exchange(0, peers, lambda pid: gs.at[pid], rs.at[me])
        if flat:
            total[...] = jnp.sum(rs[...], axis=0)
        else:
            zs[x] = jnp.sum(rs[...], axis=0)
            exchange(1, line_peers, lambda pid: zs.at[x], zs.at[x])
            total[...] = jnp.sum(zs[...], axis=0)
        keep = pltpu.make_async_copy(total, gram_hbm.at[me], ssem.at[1])
        keep.start()
        exchange(2, peers, lambda pid: total, gram_hbm.at[me])
        keep.wait()
        save.wait()

        both(ysends, lambda up: y_copies(noff, own, up, None, True), wait_send)
        both(xsends, lambda side: x_copies(noff, own, side, None, True), wait_send)
        for i in range(noff):
            slot = z_plan(i)[2]
            for c in range(nch):
                when(z_plan(i)[3], lambda i=i, c=c: wait_send(z_copies(i, c)))

                def sent(i=i, slot=slot, c=c):
                    both(ysends, lambda up: y_copies(i, slot, up, c, c == 0), wait_send)

                when(z_plan(i)[4], sent)
                both(xsends, lambda side: x_copies(i, slot, side, c, c == 0), wait_send)

    f32 = jnp.float32
    tile = (8, cols)
    group_sems = pltpu.SemaphoreType.DMA((3, max(owners, nx)))
    y_sems = pltpu.SemaphoreType.DMA((noff + 1, 2, nch + 1))
    z_sems = pltpu.SemaphoreType.DMA((noff, nch + 1))
    call = pl.pallas_call(
        kernel,
        out_shape=(
            jax.ShapeDtypeStruct((3 * leads, rows * cols), f32),
            jax.ShapeDtypeStruct((owners, share, size), f32),
        ),
        in_specs=[pl.BlockSpec(memory_space=pltpu.HBM)] * 4,
        out_specs=[pl.BlockSpec(memory_space=pltpu.HBM)] * 2,
        scratch_shapes=[
            pltpu.VMEM((3 * leads, rows * cols), f32),
            pltpu.VMEM((share, size), f32),
            pltpu.SemaphoreType.DMA((2,)),
            pltpu.SMEM((6, classes), f32),
            pltpu.VMEM((rows, cols), jnp.int32),
            pltpu.VMEM((2, leads), jnp.int32),
            pltpu.VMEM((leads * rows, cols), f32),
            pltpu.SemaphoreType.DMA((4,)),
            pltpu.VMEM((layers, ext, leads, cols), f32),
            pltpu.VMEM((layers, 3) + tile, f32),
            pltpu.VMEM((layers, ext) + tile, f32),
            pltpu.VMEM((layers,) + tile, f32),
            pltpu.VMEM((2, layers) + tile, f32),
            pltpu.VMEM((layers, leads, cols), f32),
            pltpu.VMEM((2, layers, leads, cols), f32),
            pltpu.VMEM((layers, ext) + tile, f32),
            pltpu.VMEM((layers, ext) + tile, f32),
            pltpu.VMEM((layers, rows) + tile, f32),
            pltpu.VMEM((6, layers, ext) + tile, f32),
            pltpu.VMEM((layers, ext) + tile, f32),
            pltpu.VMEM((6, layers, 2) + tile, f32),
            pltpu.VMEM((layers, 2) + tile, f32),
            pltpu.VMEM((2, leads, cols), f32),
            pltpu.VMEM((owners, share, size), f32),
            pltpu.VMEM((owners, share, size), f32),
            pltpu.VMEM((nx, share, size), f32),
            z_sems, z_sems, y_sems, y_sems, y_sems, y_sems, group_sems, group_sems,
        ],
        compiler_params=pltpu.CompilerParams(
            collective_id=0, has_side_effects=True,
            vmem_limit_bytes=VMEM_LIMIT,
        ),
        name="krylov",
    )
    return call, size


def spread_row(value, row):
    return jnp.broadcast_to(value[row : row + 1, :], (8, value.shape[1]))


def solve_four(columns, row, values, sub):
    p = [[spread_row(columns[j], row + i) for j in range(4)] for i in range(4)]
    det = p[0][0] * p[1][1] - p[0][1] * p[1][0]
    e = [
        [p[1][1] * p[0][j] - p[0][1] * p[1][j] for j in (2, 3)],
        [p[0][0] * p[1][j] - p[1][0] * p[0][j] for j in (2, 3)],
    ]
    m = [
        [det * p[i][j + 2] - (p[i][0] * e[0][j] + p[i][1] * e[1][j]) for j in range(2)]
        for i in (2, 3)
    ]
    first = 1.0 / det
    second = det / (m[0][0] * m[1][1] - m[0][1] * m[1][0])
    done = []
    for value in values:
        cut = lambda v: v[:, : value.shape[1]]
        u = [spread_row(value, row + j) for j in range(4)]
        ua = (cut(p[1][1]) * u[0] - cut(p[0][1]) * u[1]) * cut(first)
        ub = (cut(p[0][0]) * u[1] - cut(p[1][0]) * u[0]) * cut(first)
        t = [u[i] - (cut(p[i][0]) * ua + cut(p[i][1]) * ub) for i in (2, 3)]
        x2 = (cut(m[1][1]) * t[0] - cut(m[0][1]) * t[1]) * cut(second)
        x3 = (cut(m[0][0]) * t[1] - cut(m[1][0]) * t[0]) * cut(second)
        x0 = ua - (cut(e[0][0]) * x2 + cut(e[0][1]) * x3) * cut(first)
        x1 = ub - (cut(e[1][0]) * x2 + cut(e[1][1]) * x3) * cut(first)
        x = (x0, x1, x2, x3)
        value = value - (
            (cut(columns[0]) * x0 + cut(columns[1]) * x1)
            + (cut(columns[2]) * x2 + cut(columns[3]) * x3)
        )
        for j in range(4):
            value = jnp.where(cut(sub) == row + j, x[j], value)
        done.append(value)
    return done


def columns_of(tile, at):
    return [jnp.broadcast_to(tile[0][:, at + j : at + j + 1], (8, 128)) for j in range(8)]


def eliminate(matrix, count):
    width = matrix.shape[1]
    cuts = [(a, min(a + 128, width)) for a in range(0, width, 128)]
    lane = lax.broadcasted_iota(jnp.int32, (8, 128), 1)
    sub = lax.broadcasted_iota(jnp.int32, (8, 128), 0)
    tiles = []
    for i in range(0, count, 8):
        parts = [matrix[i : i + 8, a:b] for a, b in cuts]
        pivot = jnp.sum(jnp.where(lane == sub + i, parts[0], 0.0), axis=1, keepdims=True)
        inverse = 1.0 / jnp.broadcast_to(pivot, (8, 128))
        tiles.append([part * inverse[:, : part.shape[1]] for part in parts])
    for home in range(count // 8):
        soon = [home + 1] if home + 1 < len(tiles) else []
        left = {i: columns_of(tiles[i], home * 8) for i in soon}
        mine = columns_of(tiles[home], home * 8)
        parts = solve_four(mine[:4], 0, mine[4:] + tiles[home], sub)
        parts = solve_four(parts[:4], 4, parts[4:], sub)
        for i in soon:
            for h, (a, b) in enumerate(cuts):
                terms = [left[i][j][:, : b - a] * spread_row(parts[h], j) for j in range(8)]
                while len(terms) > 1:
                    terms = [terms[j] + terms[j + 1] for j in range(0, len(terms), 2)]
                tiles[i][h] = tiles[i][h] - terms[0]
        rest = [i for i in range(len(tiles)) if i != home and i not in soon]
        active = jnp.concatenate([tiles[i][0][:, :count] for i in rest], axis=0)
        solved = jnp.concatenate(parts, axis=1)
        blank = lambda n: [jnp.zeros((n, width), jnp.float32)] if n else []
        padded = jnp.concatenate(
            blank(home * 8) + [solved] + blank(count - 8 - home * 8), axis=0
        )
        change = nn_dot(active, padded)
        for n, i in enumerate(rest):
            for h, (a, b) in enumerate(cuts):
                tiles[i][h] = tiles[i][h] - change[n * 8 : n * 8 + 8, a:b]
        tiles[home] = parts
    return jnp.concatenate([jnp.concatenate(tile, axis=1) for tile in tiles], axis=0)


def make_combine(leads, rows, cols):
    def kernel(
        gram_hbm, base_hbm, field_hbm, out_hbm, res_hbm, gram, base, field, out, res, isem, osem
    ):
        loads = [
            pltpu.make_async_copy(source, target, isem.at[i])
            for i, (source, target) in enumerate(
                ((gram_hbm, gram), (base_hbm, base), (field_hbm, field))
            )
        ]
        for load in loads:
            load.start()
        loads[0].wait()
        rr, rq = gram[0:leads, 0:leads], gram[0:leads, leads : 2 * leads]
        qq, qp = gram[leads : 2 * leads, 0:leads], gram[leads : 2 * leads, leads : 2 * leads]
        first = eliminate(jnp.concatenate([rq, rr, qq], axis=1), leads)
        z2, z1 = first[:, leads : 2 * leads], first[:, 2 * leads : 3 * leads]
        schur = jnp.concatenate([qp, rq], axis=1) - nn_dot(qq, jnp.concatenate([z1, z2], axis=1))
        e = eliminate(schur, leads)[:, leads : 2 * leads]
        c = z2 - nn_dot(z1, e)
        mix = jnp.transpose(jnp.concatenate([c, e], axis=0))
        for load in loads[1:]:
            load.wait()
        gain = nn_dot(mix, base[0 : 2 * leads, :])
        for r in range(rows):
            at = slice(r * cols, (r + 1) * cols)
            spread = pl.ds(r, leads, stride=rows)
            out[spread, :] = field[spread, :] + gain[:, at]
        saves = [
            pltpu.make_async_copy(source, target, osem.at[i])
            for i, (source, target) in enumerate(((out, out_hbm), (res, res_hbm)))
        ]
        saves[0].start()
        loss = nn_dot(mix, base[leads : 3 * leads, :])
        for r in range(rows):
            at = slice(r * cols, (r + 1) * cols)
            res[pl.ds(r, leads, stride=rows), :] = base[0:leads, at] - loss[:, at]
        saves[1].start()
        for save in saves:
            save.wait()

    f32 = jnp.float32
    hbm = pl.BlockSpec(memory_space=pltpu.HBM)
    shape = jax.ShapeDtypeStruct((leads * rows, cols), f32)
    block = pltpu.VMEM((leads * rows, cols), f32)
    return pl.pallas_call(
        kernel,
        out_shape=(shape, shape),
        in_specs=[hbm] * 3,
        out_specs=(hbm, hbm),
        scratch_shapes=[
            pltpu.VMEM((2 * leads, 2 * leads), f32),
            pltpu.VMEM((3 * leads, rows * cols), f32),
            block, block, block,
            pltpu.SemaphoreType.DMA((3,)),
            pltpu.SemaphoreType.DMA((2,)),
        ],
        compiler_params=pltpu.CompilerParams(vmem_limit_bytes=VMEM_LIMIT),
        name="combine",
    )


def solution(mesh):
    nz, ny, nx = (mesh.shape[name] for name in ("gz", "gy", "gx"))

    def body(labels, tissue_tensors, electrodes, initial):
        leads, _, rows, cols = initial.shape
        field = initial.reshape(leads * rows, cols)
        krylov, size = make_krylov(
            nz, ny, nx, leads, rows, cols, tissue_tensors.shape[1]
        )
        base, gram = krylov(tissue_tensors, labels.reshape(rows, cols), electrodes, field)
        out, res = make_combine(leads, rows, cols)(gram.reshape(size, size), base, field)
        return out.reshape(initial.shape), res.reshape(initial.shape)

    placed = (P("gz", "gy", "gx"), P(), P(), P(None, "gz", "gy", "gx"))
    return jax.shard_map(
        body,
        mesh=mesh,
        in_specs=placed,
        out_specs=(P(None, "gz", "gy", "gx"), P(None, "gz", "gy", "gx")),
        check_vma=False,
    )
```

```python
import jax
import jax.numpy as jnp
from jax import lax
from jax.experimental import pallas as pl
from jax.experimental.pallas import tpu as pltpu
from jax.sharding import PartitionSpec as P

MESH = pl.DeviceIdType.MESH
HIGH = lax.Precision.HIGHEST
DEPTH = 3
CHUNKS = 2
PAIR = 1
TWIN = 4
VMEM_LIMIT = 58 * 1024 * 1024


def nt_dot(a, b):
    return lax.dot_general(
        a, b, (((1,), (1,)), ((), ())), precision=HIGH, preferred_element_type=jnp.float32
    )


def nn_dot(a, b):
    return lax.dot_general(
        a, b, (((1,), (0,)), ((), ())), precision=HIGH, preferred_element_type=jnp.float32
    )


def make_krylov(nz, ny, nx, leads, rows, cols, classes):
    windowed = nz > DEPTH + 1
    layers = 2 * DEPTH + 1 if windowed else nz
    ext = rows + 2 * DEPTH
    top = DEPTH + rows
    if windowed:
        offsets = [d for d in range(-DEPTH, DEPTH + 1) if d]
    else:
        offsets = list(range(1, nz))
    noff = len(offsets)
    groups = leads // 8
    per = groups // CHUNKS
    nch = groups // per
    span = per * 8
    plane = nz * ny
    size = 2 * leads
    share = size // plane
    last = cols - 1
    lead8 = leads + 8

    def kernel(
        table_hbm, labels_hbm, electrodes_hbm, field_hbm, base_hbm, gram_hbm,
        base_out, total, ssem, table, labels, electrodes, field, lsem,
        xe, lt, lab, xs, xr, xm, joined, re, qe, pe, coef, inside, hcoef, hinside, elec, gs, rs, zs,
        zsend, zrecv, ysend, yrecv, xsend, xrecv, asend, arecv,
    ):
        z, y, x = lax.axis_index("gz"), lax.axis_index("gy"), lax.axis_index("gx")
        own = DEPTH if windowed else z
        first = z - DEPTH if windowed else 0
        zs_ = [lax.rem(z + d, nz) for d in range(nz)]
        ys_ = [lax.rem(y + d, ny) for d in range(ny)]
        xs_ = [lax.rem(x + d, nx) for d in range(nx)]
        plane_peers = [
            (zs_[dz] * ny + ys_[dy], {"gz": zs_[dz], "gy": ys_[dy]})
            for dz in range(nz)
            for dy in range(ny)
        ]
        line_peers = [(xs_[dx], {"gx": xs_[dx]}) for dx in range(nx)]
        corner_peers = [
            (None, {"gy": ys_[dy], "gx": xs_[dx]}) for dy in (1, ny - 1) for dx in (1, nx - 1)
        ]
        greeted = plane_peers[1:] + line_peers[1:] + corner_peers

        loads = [
            pltpu.make_async_copy(source, target, lsem.at[i])
            for i, (source, target) in enumerate(
                (
                    (field_hbm, field), (labels_hbm, labels),
                    (electrodes_hbm, electrodes), (table_hbm, table),
                )
            )
        ]
        for load in loads:
            load.start()
        barrier = pltpu.get_barrier_semaphore()
        for _, device in greeted:
            pl.semaphore_signal(barrier, inc=1, device_id=device, device_id_type=MESH)

        outside = jnp.full((8, cols), -1.0, jnp.float32)

        def fill(slot, lo, hi):
            for r in range(lo, hi):
                xe[slot, r] = jnp.zeros((leads, cols), jnp.float32)

        if windowed:
            for s in range(layers):

                @pl.when((first + s < 0) | (first + s >= nz))
                def _(s=s):
                    fill(s, 0, ext)
                    for j in range(3):
                        lt[s, j] = outside
                    xm[s, 0:leads] = jnp.zeros((leads, cols), jnp.float32)
                    xm[s, leads:lead8] = outside

        for s in range(layers):

            @pl.when(y == 0)
            def _(s=s):
                fill(s, 0, DEPTH)
                lt[s, 1] = outside

            @pl.when(y == ny - 1)
            def _(s=s):
                fill(s, top, ext)
                lt[s, 2] = outside

        arrivals = (x < nx - 1, x > 0)
        beside = (y > 0, None, y < ny - 1)

        def exists(side, j):
            return arrivals[side] if j == 1 else arrivals[side] & beside[j]

        for side in (0, 1):
            for j in range(3):

                @pl.when(jnp.logical_not(exists(side, j)))
                def _(side=side, j=j):
                    xr[side, j, 0:leads] = jnp.zeros((leads, cols), jnp.float32)
                    xr[side, j, leads:lead8] = outside

        lane = lax.broadcasted_iota(jnp.int32, (8, cols), 1)

        def group(c):
            return pl.ds(pl.multiple_of(c * 8, 8), 8)

        def gather_edges(load, lo, hi):
            total = None
            for r in reversed(range(lo, hi)):
                moved = pltpu.roll(load(r), 8 * r, axis=1) if r else load(r)
                if total is None:
                    total = moved
                    continue
                keep = lane < 8 * r + DEPTH + 1
                if r == 0:
                    keep = keep | (lane >= cols - DEPTH)
                total = jnp.where(keep, moved, total)
            return total

        for load in loads:
            load.wait()
        lt[own, 0] = labels[...].astype(jnp.float32)
        for r in range(rows):
            xe[own, DEPTH + r] = field[pl.ds(r, leads, stride=rows), :]

        pl.semaphore_wait(barrier, len(greeted))

        def z_plan(i):
            d = offsets[i]
            if windowed:
                return (
                    z + d, DEPTH - d, DEPTH - d,
                    (z + d >= 0) & (z + d < nz), (z - d >= 0) & (z - d < nz),
                )
            return lax.rem(z + d, nz), z, lax.rem(z - d + nz, nz), None, None

        def when(cond, action):
            if cond is None:
                action()
            else:
                pl.when(cond)(action)

        def remote(src, dst, send, recv, device):
            return pltpu.make_async_remote_copy(
                src_ref=src, dst_ref=dst, send_sem=send, recv_sem=recv,
                device_id=device, device_id_type=MESH,
            )

        def chunk(c):
            if c is None:
                return slice(0, leads)
            if isinstance(c, int):
                return slice(c * span, (c + 1) * span)
            return pl.ds(pl.multiple_of(c * span, 8), span)

        pieces = ((DEPTH, 2 * DEPTH), (top - DEPTH, top), (2 * DEPTH, top - DEPTH))

        def z_copy(i, part, c):
            peer, slot, _, _, _ = z_plan(i)
            lo, hi = pieces[part]
            at = part * nch + c
            return remote(
                xe.at[own, lo:hi, chunk(c), :], xe.at[slot, lo:hi, chunk(c), :],
                zsend.at[i, at], zrecv.at[i, at], {"gz": peer},
            )

        def z_tile(i):
            peer, slot, _, _, _ = z_plan(i)
            return remote(
                lt.at[own, 0], lt.at[slot, 0],
                zsend.at[i, 3 * nch], zrecv.at[i, 3 * nch], {"gz": peer},
            )

        def z_rim(i):
            peer, slot, _, _, _ = z_plan(i)
            return remote(
                xm.at[own], xm.at[slot],
                zsend.at[i, 3 * nch + 1], zrecv.at[i, 3 * nch + 1], {"gz": peer},
            )

        def y_copy(i, slot, up, c):
            src = (top - DEPTH, top) if up else (DEPTH, 2 * DEPTH)
            dst = (0, DEPTH) if up else (top, ext)
            at = 0 if c is None else c
            return remote(
                xe.at[slot, src[0] : src[1], chunk(c), :],
                xe.at[slot, dst[0] : dst[1], chunk(c), :],
                ysend.at[i, up, at], yrecv.at[i, up, at], {"gy": y + 1 if up else y - 1},
            )

        def y_tile(i, slot, up):
            return remote(
                lt.at[slot, 0], lt.at[slot, 1 if up else 2],
                ysend.at[i, up, nch], yrecv.at[i, up, nch], {"gy": y + 1 if up else y - 1},
            )

        def x_copy(side, j):
            return remote(
                xs, xr.at[side, j], xsend.at[side, j], xrecv.at[side, j],
                {"gx": x + 1 if side else x - 1, "gy": y + (1 - j)},
            )

        has_low, has_high = y > 0, y < ny - 1
        ysends = (has_low, has_high)
        xsends = (x > 0, x < nx - 1)

        def y_each(action, make):
            for up in (1, 0):
                pl.when(ysends[up])(lambda up=up: action(make(up)))

        def y_arrive(make):
            for up in (1, 0):
                pl.when(ysends[1 - up])(lambda up=up: make(up).wait_recv())

        def x_each(action):
            for j in (1, 0, 2):
                for side in (0, 1):
                    there = xsends[side] if j == 1 else xsends[side] & ysends[1 - j // 2]
                    pl.when(there)(lambda side=side, j=j: action(x_copy(side, j)))

        def begin(copy):
            copy.start()

        def z_start(make):
            for i in range(noff):
                when(z_plan(i)[3], lambda i=i: make(i).start())

        z_start(z_tile)
        z_start(lambda i: z_copy(i, 0, 0))
        z_start(lambda i: z_copy(i, 1, 0))
        for c in range(groups):
            xs[c * 8 : c * 8 + 8, :] = gather_edges(
                lambda r: xe[own, r, c * 8 : c * 8 + 8, :], DEPTH, top
            )
        xs[leads:lead8] = gather_edges(
            lambda r: jnp.broadcast_to(lt[own, 0, r - DEPTH : r - DEPTH + 1, :], (8, cols)),
            DEPTH, top,
        )
        x_each(begin)
        y_each(begin, lambda up: y_copy(noff, own, up, None))
        y_each(begin, lambda up: y_tile(noff, own, up))
        for c in range(1, nch):
            for part in (0, 1):
                z_start(lambda i: z_copy(i, part, c))
        for c in range(nch - 1):
            z_start(lambda i: z_copy(i, 2, c))

        eye = lax.broadcasted_iota(jnp.int32, (leads, leads), 0) == lax.broadcasted_iota(
            jnp.int32, (leads, leads), 1
        )
        for e in range(2):
            line = electrodes[e : e + 1, :].astype(jnp.float32)
            column = jnp.sum(
                jnp.where(eye, jnp.broadcast_to(line, (leads, leads)), 0.0), axis=1, keepdims=True
            )
            elec[e] = jnp.broadcast_to(column, (leads, cols))

        near = (lane & 7) < 4
        middle = (lane >= 8 * DEPTH - DEPTH) & (lane < 8 * top - DEPTH)

        def forward(c):
            for part in (0, 1):
                for i in range(noff):

                    def arrived(i=i, part=part):
                        z_copy(i, part, c).wait_recv()
                        pl.when(ysends[part])(
                            lambda: y_copy(i, z_plan(i)[2], part, c).start()
                        )

                    when(z_plan(i)[4], arrived)

        for i in range(noff):

            def arrived(i=i):
                z_tile(i).wait_recv()
                y_each(begin, lambda up: y_tile(i, z_plan(i)[2], up))

            when(z_plan(i)[4], arrived)
        forward(0)

        for side in (0, 1):
            for j in range(3):
                pl.when(exists(side, j))(lambda side=side, j=j: x_copy(side, j).wait_recv())

        for c in range(lead8 // 8):
            at = slice(c * 8, c * 8 + 8)
            sides = [jnp.where(near, xr[0, j, at, :], xr[1, j, at, :]) for j in range(3)]
            corners = jnp.where(lane < 8 * DEPTH + 28, sides[2], sides[0])
            xm[own, at, :] = jnp.where(middle, sides[1], pltpu.roll(corners, 8 * rows, axis=1))

        z_start(z_rim)
        z_start(lambda i: z_copy(i, 2, nch - 1))
        for c in range(1, nch):
            forward(c)

        y_arrive(lambda up: y_tile(noff, own, up))
        for i in range(noff):
            when(z_plan(i)[4], lambda i=i: y_arrive(lambda up: y_tile(i, z_plan(i)[2], up)))

        for s in range(layers):
            for r in range(ext):
                if r < DEPTH:
                    row = lt[s, 1, rows - DEPTH + r : rows - DEPTH + r + 1, :]
                elif r < top:
                    row = lt[s, 0, r - DEPTH : r - DEPTH + 1, :]
                else:
                    row = lt[s, 2, r - top : r - top + 1, :]
                lab[s, r] = jnp.broadcast_to(row, (8, cols))

        values = [[table[i, t] for t in range(table.shape[1])] for i in range(6)]

        def look(label):
            parts = [jnp.zeros(label.shape, jnp.float32)] * 6
            for t in range(table.shape[1]):
                match = label == float(t)
                parts = [jnp.where(match, values[i][t], parts[i]) for i in range(6)]
            return parts, jnp.where(label >= 0.0, 1.0, 0.0)

        def lookup(r, _):
            for s in range(layers):
                parts, here = look(lab[s, r])
                for i in range(6):
                    coef[i, s, r] = parts[i]
                inside[s, r] = here
            return 0

        lax.fori_loop(0, ext, lookup, 0)
        edges = [gather_edges(lambda r: lab[s, r], 0, ext) for s in range(layers)]
        y_arrive(lambda up: y_copy(noff, own, up, None))
        for i in range(noff):
            when(z_plan(i)[4], lambda i=i: z_rim(i).wait_recv())
        for s in range(layers):
            for side in (0, 1):
                beyond = xm[s, leads:lead8, :]
                label = (
                    jnp.where(near, edges[s], beyond) if side else jnp.where(near, beyond, edges[s])
                )
                parts, here = look(label)
                for i in range(6):
                    hcoef[i, s, side] = parts[i]
                hinside[s, side] = here

        line_width = nx * cols
        column = (x * cols + lane).astype(jnp.float32)
        moved = jnp.where(lane >= cols - DEPTH, lane + DEPTH - cols, lane + DEPTH)
        packed_row = moved // 8
        packed_voxel = packed_row * line_width + (moved - packed_row * 8) + (
            x * cols + (y * rows - DEPTH) * line_width - DEPTH
        )
        ends = (lane == 0, lane == last)
        seam = (lane & 7) == 7

        def source(c, voxel):
            return jnp.where(
                elec[0, group(c), :] == voxel, 1.0,
                jnp.where(elec[1, group(c), :] == voxel, -1.0, 0.0),
            )

        def flux(t, axis, grads):
            order = ((0, 3, 4), (3, 1, 5), (4, 5, 2))[axis]
            return t[order[0]] * grads[0] + t[order[1]] * grads[1] + t[order[2]] * grads[2]

        def rim(fields, side, full):
            sums, edges = [], []
            below = None
            for s in range(layers):
                t = [hcoef[i, s, side] for i in range(6)]
                v = fields[s]
                grads = (
                    pltpu.roll(v, last, axis=1) - v,
                    pltpu.roll(v, cols - 8, axis=1) - v,
                    fields[s + 1] - v if s + 1 < layers else -v,
                )
                flux_x = flux(t, 0, grads)
                edges.append(flux_x)
                if full:
                    flux_y, flux_z = flux(t, 1, grads), flux(t, 2, grads)
                    total = (pltpu.roll(flux_y, 8, axis=1) - flux_y) + (
                        pltpu.roll(flux_x, 1, axis=1) - flux_x
                    )
                    total = total - flux_z if below is None else total + (below - flux_z)
                    below = flux_z
                    sums.append(total)
            return sums, edges

        def seams(right, edges):
            return [
                jnp.where(seam, edges[s], pltpu.roll(right[s], cols - 2, axis=1))
                for s in range(layers)
            ]

        def operate(load, emit, lo, hi, joins, count):
            below_y = [[None] * layers for _ in range(count)]
            for r in range(lo - 1, hi):
                here = [[load(k, s, r) for s in range(layers)] for k in range(count)]
                below_z = [None] * count
                for s in range(layers):
                    t = [coef[i, s, r] for i in range(6)]
                    for k in range(count):
                        v = here[k][s]
                        join = pltpu.roll(joins[k][s], (cols + 1 - 8 * r) % cols, axis=1)
                        grads = (
                            jnp.where(ends[1], join, pltpu.roll(v, last, axis=1)) - v,
                            load(k, s, r + 1) - v,
                            here[k][s + 1] - v if s + 1 < layers else -v,
                        )
                        flux_y = flux(t, 1, grads)
                        if r >= lo:
                            flux_x, flux_z = flux(t, 0, grads), flux(t, 2, grads)
                            before = jnp.where(ends[0], join, pltpu.roll(flux_x, 1, axis=1))
                            total = (below_y[k][s] - flux_y) + (before - flux_x)
                            total = total - flux_z if s == 0 else total + (below_z[k] - flux_z)
                            emit(k, s, r, total)
                            below_z[k] = flux_z
                        below_y[k][s] = flux_y

        def clip(value, s, r):
            return value if not windowed and DEPTH <= r < top else value * inside[s, r]

        plane_voxels = ny * rows * line_width

        def rims(c):
            mine = [
                gather_edges(lambda r: xe[s, r, group(c), :], 0, ext) for s in range(layers)
            ]
            beyond = [xm[s, group(c), :] for s in range(layers)]
            right = [jnp.where(near, beyond[s], mine[s]) for s in range(layers)]
            left = [jnp.where(near, mine[s], beyond[s]) for s in range(layers)]

            def keep(n, joins):
                for s in range(layers):
                    joined[n, s, group(c), :] = joins[s]

            right_sum, _ = rim(right, 0, True)
            left_sum, left_edge = rim(left, 1, True)
            keep(0, seams(right, left_edge))

            def rim_r(total, s, side):
                voxel = packed_voxel + ((first + s) * plane_voxels + (0 if side else cols))
                return (source(c, voxel.astype(jnp.float32)) - total) * hinside[s, side]

            right_r = [rim_r(right_sum[s], s, 0) for s in range(layers)]
            left_r = [rim_r(left_sum[s], s, 1) for s in range(layers)]
            right_sum, _ = rim(right_r, 0, True)
            left_sum, left_edge = rim(left_r, 1, True)
            keep(1, seams(right_r, left_edge))
            right_q = [right_sum[s] * hinside[s, 0] for s in range(layers)]
            left_q = [left_sum[s] * hinside[s, 1] for s in range(layers)]
            _, left_edge = rim(left_q, 1, False)
            keep(2, seams(right_q, left_edge))

        def advance(cs):
            def joins_of(n, c):
                return [joined[n, s, group(c), :] for s in range(layers)]

            def emit_r(k, s, r, total):
                row = (first + s) * (ny * rows) + y * rows + (r - DEPTH)
                voxel = column + (row * line_width).astype(jnp.float32)
                re[k, s, r] = clip(source(cs[k], voxel) - total, s, r)

            def emit_q(k, s, r, total):
                qe[k, s, r] = clip(total, s, r)

            def emit_p(k, s, r, total):
                pe[k, s, r - DEPTH] = total

            def field_of(k, s, r):
                return xe[s, r, group(cs[k]), :]

            count = len(cs)
            joins = [[joins_of(n, c) for c in cs] for n in range(3)]
            operate(field_of, emit_r, 1, ext - 1, joins[0], count)
            operate(lambda k, s, r: re[k, s, r], emit_q, 2, ext - 2, joins[1], count)
            operate(lambda k, s, r: qe[k, s, r], emit_p, 3, ext - 3, joins[2], count)
            for k, c in enumerate(cs):
                for r in range(rows):
                    at = slice(r * cols, (r + 1) * cols)
                    base_out[group(c), at] = re[k, own, DEPTH + r]
                    base_out[group(c + groups), at] = qe[k, own, DEPTH + r]
                    base_out[group(c + 2 * groups), at] = pe[k, own, r]

        def turn(c, _):
            for i in range(noff):

                def arrived(i=i):
                    z_copy(i, 2, c).wait_recv()
                    y_arrive(lambda up: y_copy(i, z_plan(i)[2], up, c))

                when(z_plan(i)[4], arrived)

            def edge(g, _):
                for k in range(TWIN):
                    rims(c * per + g * TWIN + k)
                return 0

            lax.fori_loop(0, per // TWIN, edge, 0)

            def step(g, _):
                advance([c * per + g * PAIR + k for k in range(PAIR)])
                return 0

            lax.fori_loop(0, per // PAIR, step, 0)
            return 0

        lax.fori_loop(0, nch, turn, 0)

        upper = nt_dot(base_out[0:leads, :], base_out[0 : 2 * leads, :])
        lower = nt_dot(base_out[leads : 2 * leads, :], base_out[leads : 3 * leads, :])
        grams = jnp.concatenate([upper, lower], axis=0)
        for i in range(plane):
            gs[i] = grams[i * share : (i + 1) * share, :]

        save = pltpu.make_async_copy(base_out, base_hbm, ssem.at[0])
        save.start()

        def exchange(phase, peers, source_of, target):
            copies = [
                remote(source_of(pid), target, asend.at[phase, k], arecv.at[phase, k], device)
                for k, (pid, device) in enumerate(peers)
                if k
            ]
            for copy in copies:
                copy.start()
            for copy in copies:
                copy.wait()

        me = plane_peers[0][0]
        rs[me] = gs[me]
        exchange(0, plane_peers, lambda pid: gs.at[pid], rs.at[me])
        zs[x] = jnp.sum(rs[...], axis=0)
        exchange(1, line_peers, lambda pid: zs.at[x], zs.at[x])
        total[...] = jnp.sum(zs[...], axis=0)
        keep = pltpu.make_async_copy(total, gram_hbm.at[me], ssem.at[1])
        keep.start()
        exchange(2, plane_peers, lambda pid: total, gram_hbm.at[me])
        keep.wait()
        save.wait()

        def sent(copy):
            copy.wait_send()

        y_each(sent, lambda up: y_copy(noff, own, up, None))
        y_each(sent, lambda up: y_tile(noff, own, up))
        x_each(sent)
        for i in range(noff):
            for part in range(3):
                for c in range(nch):
                    when(z_plan(i)[3], lambda i=i, part=part, c=c: sent(z_copy(i, part, c)))
            when(z_plan(i)[3], lambda i=i: sent(z_tile(i)))
            when(z_plan(i)[3], lambda i=i: sent(z_rim(i)))

            def forwarded(i=i):
                slot = z_plan(i)[2]
                for c in range(nch):
                    y_each(sent, lambda up: y_copy(i, slot, up, c))
                y_each(sent, lambda up: y_tile(i, slot, up))

            when(z_plan(i)[4], forwarded)

    f32 = jnp.float32
    tile = (8, cols)
    group_sems = pltpu.SemaphoreType.DMA((3, max(plane, nx)))
    y_sems = pltpu.SemaphoreType.DMA((noff + 1, 2, nch + 1))
    z_sems = pltpu.SemaphoreType.DMA((noff, 3 * nch + 2))
    x_sems = pltpu.SemaphoreType.DMA((2, 3))
    call = pl.pallas_call(
        kernel,
        out_shape=(
            jax.ShapeDtypeStruct((3 * leads, rows * cols), f32),
            jax.ShapeDtypeStruct((plane, share, size), f32),
        ),
        in_specs=[pl.BlockSpec(memory_space=pltpu.HBM)] * 4,
        out_specs=[pl.BlockSpec(memory_space=pltpu.HBM)] * 2,
        scratch_shapes=[
            pltpu.VMEM((3 * leads, rows * cols), f32),
            pltpu.VMEM((share, size), f32),
            pltpu.SemaphoreType.DMA((2,)),
            pltpu.SMEM((6, classes), f32),
            pltpu.VMEM((rows, cols), jnp.int32),
            pltpu.VMEM((2, leads), jnp.int32),
            pltpu.VMEM((leads * rows, cols), f32),
            pltpu.SemaphoreType.DMA((4,)),
            pltpu.VMEM((layers, ext, leads, cols), f32),
            pltpu.VMEM((layers, 3) + tile, f32),
            pltpu.VMEM((layers, ext) + tile, f32),
            pltpu.VMEM((lead8, cols), f32),
            pltpu.VMEM((2, 3, lead8, cols), f32),
            pltpu.VMEM((layers, lead8, cols), f32),
            pltpu.VMEM((3, layers, leads, cols), f32),
            pltpu.VMEM((PAIR, layers, ext) + tile, f32),
            pltpu.VMEM((PAIR, layers, ext) + tile, f32),
            pltpu.VMEM((PAIR, layers, rows) + tile, f32),
            pltpu.VMEM((6, layers, ext) + tile, f32),
            pltpu.VMEM((layers, ext) + tile, f32),
            pltpu.VMEM((6, layers, 2) + tile, f32),
            pltpu.VMEM((layers, 2) + tile, f32),
            pltpu.VMEM((2, leads, cols), f32),
            pltpu.VMEM((plane, share, size), f32),
            pltpu.VMEM((plane, share, size), f32),
            pltpu.VMEM((nx, share, size), f32),
            z_sems, z_sems, y_sems, y_sems, x_sems, x_sems, group_sems, group_sems,
        ],
        compiler_params=pltpu.CompilerParams(
            collective_id=0, has_side_effects=True,
            vmem_limit_bytes=VMEM_LIMIT,
        ),
        name="krylov",
    )
    return call, size


def spread_row(value, row):
    return jnp.broadcast_to(value[row : row + 1, :], (8, value.shape[1]))


def solve_four(columns, row, values, sub):
    p = [[spread_row(columns[j], row + i) for j in range(4)] for i in range(4)]
    det = p[0][0] * p[1][1] - p[0][1] * p[1][0]
    e = [
        [p[1][1] * p[0][j] - p[0][1] * p[1][j] for j in (2, 3)],
        [p[0][0] * p[1][j] - p[1][0] * p[0][j] for j in (2, 3)],
    ]
    m = [
        [det * p[i][j + 2] - (p[i][0] * e[0][j] + p[i][1] * e[1][j]) for j in range(2)]
        for i in (2, 3)
    ]
    first = 1.0 / det
    second = det / (m[0][0] * m[1][1] - m[0][1] * m[1][0])
    done = []
    for value in values:
        cut = lambda v: v[:, : value.shape[1]]
        u = [spread_row(value, row + j) for j in range(4)]
        ua = (cut(p[1][1]) * u[0] - cut(p[0][1]) * u[1]) * cut(first)
        ub = (cut(p[0][0]) * u[1] - cut(p[1][0]) * u[0]) * cut(first)
        t = [u[i] - (cut(p[i][0]) * ua + cut(p[i][1]) * ub) for i in (2, 3)]
        x2 = (cut(m[1][1]) * t[0] - cut(m[0][1]) * t[1]) * cut(second)
        x3 = (cut(m[0][0]) * t[1] - cut(m[1][0]) * t[0]) * cut(second)
        x0 = ua - (cut(e[0][0]) * x2 + cut(e[0][1]) * x3) * cut(first)
        x1 = ub - (cut(e[1][0]) * x2 + cut(e[1][1]) * x3) * cut(first)
        x = (x0, x1, x2, x3)
        value = value - (
            (cut(columns[0]) * x0 + cut(columns[1]) * x1)
            + (cut(columns[2]) * x2 + cut(columns[3]) * x3)
        )
        for j in range(4):
            value = jnp.where(cut(sub) == row + j, x[j], value)
        done.append(value)
    return done


def columns_of(tile, at):
    return [jnp.broadcast_to(tile[0][:, at + j : at + j + 1], (8, 128)) for j in range(8)]


def eliminate(matrix, count):
    width = matrix.shape[1]
    cuts = [(a, min(a + 128, width)) for a in range(0, width, 128)]
    lane = lax.broadcasted_iota(jnp.int32, (8, 128), 1)
    sub = lax.broadcasted_iota(jnp.int32, (8, 128), 0)
    tiles = []
    for i in range(0, count, 8):
        parts = [matrix[i : i + 8, a:b] for a, b in cuts]
        pivot = jnp.sum(jnp.where(lane == sub + i, parts[0], 0.0), axis=1, keepdims=True)
        inverse = 1.0 / jnp.broadcast_to(pivot, (8, 128))
        tiles.append([part * inverse[:, : part.shape[1]] for part in parts])
    for home in range(count // 8):
        soon = [home + 1] if home + 1 < len(tiles) else []
        left = {i: columns_of(tiles[i], home * 8) for i in soon}
        mine = columns_of(tiles[home], home * 8)
        parts = solve_four(mine[:4], 0, mine[4:] + tiles[home], sub)
        parts = solve_four(parts[:4], 4, parts[4:], sub)
        for i in soon:
            for h, (a, b) in enumerate(cuts):
                terms = [left[i][j][:, : b - a] * spread_row(parts[h], j) for j in range(8)]
                while len(terms) > 1:
                    terms = [terms[j] + terms[j + 1] for j in range(0, len(terms), 2)]
                tiles[i][h] = tiles[i][h] - terms[0]
        rest = [i for i in range(len(tiles)) if i != home and i not in soon]
        active = jnp.concatenate([tiles[i][0][:, :count] for i in rest], axis=0)
        solved = jnp.concatenate(parts, axis=1)
        blank = lambda n: [jnp.zeros((n, width), jnp.float32)] if n else []
        padded = jnp.concatenate(
            blank(home * 8) + [solved] + blank(count - 8 - home * 8), axis=0
        )
        change = nn_dot(active, padded)
        for n, i in enumerate(rest):
            for h, (a, b) in enumerate(cuts):
                tiles[i][h] = tiles[i][h] - change[n * 8 : n * 8 + 8, a:b]
        tiles[home] = parts
    return jnp.concatenate([jnp.concatenate(tile, axis=1) for tile in tiles], axis=0)


def make_combine(leads, rows, cols):
    def kernel(
        gram_hbm, base_hbm, field_hbm, out_hbm, res_hbm, gram, base, field, out, res, isem, osem
    ):
        loads = [
            pltpu.make_async_copy(source, target, isem.at[i])
            for i, (source, target) in enumerate(
                ((gram_hbm, gram), (base_hbm, base), (field_hbm, field))
            )
        ]
        for load in loads:
            load.start()
        loads[0].wait()
        rr, rq = gram[0:leads, 0:leads], gram[0:leads, leads : 2 * leads]
        qq, qp = gram[leads : 2 * leads, 0:leads], gram[leads : 2 * leads, leads : 2 * leads]
        first = eliminate(jnp.concatenate([rq, rr, qq], axis=1), leads)
        z2, z1 = first[:, leads : 2 * leads], first[:, 2 * leads : 3 * leads]
        schur = jnp.concatenate([qp, rq], axis=1) - nn_dot(qq, jnp.concatenate([z1, z2], axis=1))
        e = eliminate(schur, leads)[:, leads : 2 * leads]
        c = z2 - nn_dot(z1, e)
        mix = jnp.transpose(jnp.concatenate([c, e], axis=0))
        for load in loads[1:]:
            load.wait()
        gain = nn_dot(mix, base[0 : 2 * leads, :])
        for r in range(rows):
            at = slice(r * cols, (r + 1) * cols)
            spread = pl.ds(r, leads, stride=rows)
            out[spread, :] = field[spread, :] + gain[:, at]
        saves = [
            pltpu.make_async_copy(source, target, osem.at[i])
            for i, (source, target) in enumerate(((out, out_hbm), (res, res_hbm)))
        ]
        saves[0].start()
        loss = nn_dot(mix, base[leads : 3 * leads, :])
        for r in range(rows):
            at = slice(r * cols, (r + 1) * cols)
            res[pl.ds(r, leads, stride=rows), :] = base[0:leads, at] - loss[:, at]
        saves[1].start()
        for save in saves:
            save.wait()

    f32 = jnp.float32
    hbm = pl.BlockSpec(memory_space=pltpu.HBM)
    shape = jax.ShapeDtypeStruct((leads * rows, cols), f32)
    block = pltpu.VMEM((leads * rows, cols), f32)
    return pl.pallas_call(
        kernel,
        out_shape=(shape, shape),
        in_specs=[hbm] * 3,
        out_specs=(hbm, hbm),
        scratch_shapes=[
            pltpu.VMEM((2 * leads, 2 * leads), f32),
            pltpu.VMEM((3 * leads, rows * cols), f32),
            block, block, block,
            pltpu.SemaphoreType.DMA((3,)),
            pltpu.SemaphoreType.DMA((2,)),
        ],
        compiler_params=pltpu.CompilerParams(vmem_limit_bytes=VMEM_LIMIT),
        name="combine",
    )


def solution(mesh):
    nz, ny, nx = (mesh.shape[name] for name in ("gz", "gy", "gx"))

    def body(labels, tissue_tensors, electrodes, initial):
        leads, _, rows, cols = initial.shape
        field = initial.reshape(leads * rows, cols)
        krylov, size = make_krylov(
            nz, ny, nx, leads, rows, cols, tissue_tensors.shape[1]
        )
        base, gram = krylov(tissue_tensors, labels.reshape(rows, cols), electrodes, field)
        out, res = make_combine(leads, rows, cols)(gram.reshape(size, size), base, field)
        return out.reshape(initial.shape), res.reshape(initial.shape)

    placed = (P("gz", "gy", "gx"), P(), P(), P(None, "gz", "gy", "gx"))
    return jax.shard_map(
        body,
        mesh=mesh,
        in_specs=placed,
        out_specs=(P(None, "gz", "gy", "gx"), P(None, "gz", "gy", "gx")),
        check_vma=False,
    )
```

```python
import jax
import jax.numpy as jnp
from jax import lax
from jax.experimental import pallas as pl
from jax.experimental.pallas import tpu as pltpu
from jax.sharding import PartitionSpec as P

MESH = pl.DeviceIdType.MESH
HIGH = lax.Precision.HIGHEST
DEPTH = 3
CHUNKS = 4
PAIR = 2
TWIN = 2
VMEM_LIMIT = 58 * 1024 * 1024


def nt_dot(a, b):
    return lax.dot_general(
        a, b, (((1,), (1,)), ((), ())), precision=HIGH, preferred_element_type=jnp.float32
    )


def nn_dot(a, b):
    return lax.dot_general(
        a, b, (((1,), (0,)), ((), ())), precision=HIGH, preferred_element_type=jnp.float32
    )


def make_krylov(nz, ny, nx, leads, rows, cols, classes):
    windowed = nz > DEPTH + 1
    layers = 2 * DEPTH + 1 if windowed else nz
    ext = rows + 2 * DEPTH
    top = DEPTH + rows
    if windowed:
        offsets = [d for d in range(-DEPTH, DEPTH + 1) if d]
    else:
        offsets = list(range(1, nz))
    noff = len(offsets)
    groups = leads // 8
    per = groups // CHUNKS
    nch = groups // per
    span = per * 8
    plane = nz * ny
    size = 2 * leads
    share = size // plane
    last = cols - 1
    lead8 = leads + 8

    def kernel(
        table_hbm, labels_hbm, electrodes_hbm, field_hbm, base_hbm, gram_hbm,
        base_out, total, ssem, table, labels, electrodes, field, lsem,
        xe, lt, lab, lp, xs, xr, xm, xp, xq, joined, re, qe, pe, coef, inside, hcoef, hinside, elec, gs, rs, zs,
        zsend, zrecv, ysend, yrecv, xsend, xrecv, asend, arecv,
    ):
        z, y, x = lax.axis_index("gz"), lax.axis_index("gy"), lax.axis_index("gx")
        own = DEPTH if windowed else z
        first = z - DEPTH if windowed else 0
        zs_ = [lax.rem(z + d, nz) for d in range(nz)]
        ys_ = [lax.rem(y + d, ny) for d in range(ny)]
        xs_ = [lax.rem(x + d, nx) for d in range(nx)]
        plane_peers = [
            (zs_[dz] * ny + ys_[dy], {"gz": zs_[dz], "gy": ys_[dy]})
            for dz in range(nz)
            for dy in range(ny)
        ]
        line_peers = [(xs_[dx], {"gx": xs_[dx]}) for dx in range(nx)]
        corner_peers = [
            (None, {"gy": ys_[dy], "gx": xs_[dx]}) for dy in (1, ny - 1) for dx in (1, nx - 1)
        ]
        greeted = plane_peers[1:] + line_peers[1:] + corner_peers

        loads = [
            pltpu.make_async_copy(source, target, lsem.at[i])
            for i, (source, target) in enumerate(
                (
                    (field_hbm, field), (labels_hbm, labels),
                    (electrodes_hbm, electrodes), (table_hbm, table),
                )
            )
        ]
        for load in loads:
            load.start()
        barrier = pltpu.get_barrier_semaphore()
        for _, device in greeted:
            pl.semaphore_signal(barrier, inc=1, device_id=device, device_id_type=MESH)

        outside = jnp.full((8, cols), -1.0, jnp.float32)

        def fill(slot, lo, hi):
            for r in range(lo, hi):
                xe[slot, r] = jnp.zeros((leads, cols), jnp.float32)

        if windowed:
            for s in range(layers):

                @pl.when((first + s < 0) | (first + s >= nz))
                def _(s=s):
                    fill(s, 0, ext)
                    for j in range(3):
                        lt[s, j] = outside
                    xm[s, 0:leads] = jnp.zeros((leads, cols), jnp.float32)
                    xm[s, leads:lead8] = outside

        for s in range(layers):

            @pl.when(y == 0)
            def _(s=s):
                fill(s, 0, DEPTH)
                lt[s, 1] = outside

            @pl.when(y == ny - 1)
            def _(s=s):
                fill(s, top, ext)
                lt[s, 2] = outside

        arrivals = (x < nx - 1, x > 0)
        beside = (y > 0, None, y < ny - 1)

        def exists(side, j):
            return arrivals[side] if j == 1 else arrivals[side] & beside[j]

        for side in (0, 1):
            for j in range(3):

                @pl.when(jnp.logical_not(exists(side, j)))
                def _(side=side, j=j):
                    xr[side, j, 0:leads] = jnp.zeros((leads, cols), jnp.float32)
                    xr[side, j, leads:lead8] = outside

        lane = lax.broadcasted_iota(jnp.int32, (8, cols), 1)

        def group(c):
            return pl.ds(pl.multiple_of(c * 8, 8), 8)

        def gather_edges(load, lo, hi):
            total = None
            for r in reversed(range(lo, hi)):
                moved = pltpu.roll(load(r), 8 * r, axis=1) if r else load(r)
                if total is None:
                    total = moved
                    continue
                keep = lane < 8 * r + DEPTH + 1
                if r == 0:
                    keep = keep | (lane >= cols - DEPTH)
                total = jnp.where(keep, moved, total)
            return total

        for load in loads:
            load.wait()
        lt[own, 0] = labels[...].astype(jnp.float32)
        for r in range(rows):
            xe[own, DEPTH + r] = field[pl.ds(r, leads, stride=rows), :]

        pl.semaphore_wait(barrier, len(greeted))

        def z_plan(i):
            d = offsets[i]
            if windowed:
                return (
                    z + d, DEPTH - d, DEPTH - d,
                    (z + d >= 0) & (z + d < nz), (z - d >= 0) & (z - d < nz),
                )
            return lax.rem(z + d, nz), z, lax.rem(z - d + nz, nz), None, None

        def when(cond, action):
            if cond is None:
                action()
            else:
                pl.when(cond)(action)

        def remote(src, dst, send, recv, device):
            return pltpu.make_async_remote_copy(
                src_ref=src, dst_ref=dst, send_sem=send, recv_sem=recv,
                device_id=device, device_id_type=MESH,
            )

        def chunk(c):
            if c is None:
                return slice(0, leads)
            if isinstance(c, int):
                return slice(c * span, (c + 1) * span)
            return pl.ds(pl.multiple_of(c * span, 8), span)

        pieces = ((DEPTH, 2 * DEPTH), (top - DEPTH, top), (2 * DEPTH, top - DEPTH))

        def z_copy(i, part, c):
            peer, slot, _, _, _ = z_plan(i)
            lo, hi = pieces[part]
            at = part * nch + c
            return remote(
                xe.at[own, lo:hi, chunk(c), :], xe.at[slot, lo:hi, chunk(c), :],
                zsend.at[i, at], zrecv.at[i, at], {"gz": peer},
            )

        def z_tile(i):
            peer, slot, _, _, _ = z_plan(i)
            return remote(
                lt.at[own, 0], lt.at[slot, 0],
                zsend.at[i, 3 * nch], zrecv.at[i, 3 * nch], {"gz": peer},
            )

        def z_rim(i):
            peer, slot, _, _, _ = z_plan(i)
            return remote(
                xm.at[own], xm.at[slot],
                zsend.at[i, 3 * nch + 1], zrecv.at[i, 3 * nch + 1], {"gz": peer},
            )

        def y_copy(i, slot, up, c):
            src = (top - DEPTH, top) if up else (DEPTH, 2 * DEPTH)
            dst = (0, DEPTH) if up else (top, ext)
            at = 0 if c is None else c
            return remote(
                xe.at[slot, src[0] : src[1], chunk(c), :],
                xe.at[slot, dst[0] : dst[1], chunk(c), :],
                ysend.at[i, up, at], yrecv.at[i, up, at], {"gy": y + 1 if up else y - 1},
            )

        def y_tile(i, slot, up):
            return remote(
                lt.at[slot, 0], lt.at[slot, 1 if up else 2],
                ysend.at[i, up, nch], yrecv.at[i, up, nch], {"gy": y + 1 if up else y - 1},
            )

        def x_copy(side, j):
            return remote(
                xs, xr.at[side, j], xsend.at[side, j], xrecv.at[side, j],
                {"gx": x + 1 if side else x - 1, "gy": y + (1 - j)},
            )

        has_low, has_high = y > 0, y < ny - 1
        ysends = (has_low, has_high)
        xsends = (x > 0, x < nx - 1)

        def y_each(action, make):
            for up in (1, 0):
                pl.when(ysends[up])(lambda up=up: action(make(up)))

        def y_arrive(make):
            for up in (1, 0):
                pl.when(ysends[1 - up])(lambda up=up: make(up).wait_recv())

        def x_each(action):
            for j in (1, 0, 2):
                for side in (0, 1):
                    there = xsends[side] if j == 1 else xsends[side] & ysends[1 - j // 2]
                    pl.when(there)(lambda side=side, j=j: action(x_copy(side, j)))

        def begin(copy):
            copy.start()

        def z_start(make):
            for i in range(noff):
                when(z_plan(i)[3], lambda i=i: make(i).start())

        z_start(z_tile)
        z_start(lambda i: z_copy(i, 0, 0))
        z_start(lambda i: z_copy(i, 1, 0))
        for c in range(groups):
            xs[c * 8 : c * 8 + 8, :] = gather_edges(
                lambda r: xe[own, r, c * 8 : c * 8 + 8, :], DEPTH, top
            )
        xs[leads:lead8] = gather_edges(
            lambda r: jnp.broadcast_to(lt[own, 0, r - DEPTH : r - DEPTH + 1, :], (8, cols)),
            DEPTH, top,
        )
        x_each(begin)
        y_each(begin, lambda up: y_copy(noff, own, up, None))
        y_each(begin, lambda up: y_tile(noff, own, up))
        for c in range(1, nch):
            for part in (0, 1):
                z_start(lambda i: z_copy(i, part, c))
        for c in range(nch // 2):
            z_start(lambda i: z_copy(i, 2, c))

        eye = lax.broadcasted_iota(jnp.int32, (leads, leads), 0) == lax.broadcasted_iota(
            jnp.int32, (leads, leads), 1
        )
        for e in range(2):
            line = electrodes[e : e + 1, :].astype(jnp.float32)
            column = jnp.sum(
                jnp.where(eye, jnp.broadcast_to(line, (leads, leads)), 0.0), axis=1, keepdims=True
            )
            elec[e] = jnp.broadcast_to(column, (leads, cols))

        near = (lane & 7) < 4
        middle = (lane >= 8 * DEPTH - DEPTH) & (lane < 8 * top - DEPTH)

        def forward(c):
            for part in (0, 1):
                for i in range(noff):

                    def arrived(i=i, part=part):
                        z_copy(i, part, c).wait_recv()
                        pl.when(ysends[part])(
                            lambda: y_copy(i, z_plan(i)[2], part, c).start()
                        )

                    when(z_plan(i)[4], arrived)

        for i in range(noff):

            def arrived(i=i):
                z_tile(i).wait_recv()
                y_each(begin, lambda up: y_tile(i, z_plan(i)[2], up))

            when(z_plan(i)[4], arrived)
        forward(0)

        values = [[table[i, t] for t in range(table.shape[1])] for i in range(6)]

        def look(label):
            parts = [jnp.zeros(label.shape, jnp.float32)] * 6
            for t in range(table.shape[1]):
                match = label == float(t)
                parts = [jnp.where(match, values[i][t], parts[i]) for i in range(6)]
            return parts, jnp.where(label >= 0.0, 1.0, 0.0)

        def prepare(slot, c):
            xp[slot, group(c), :] = gather_edges(lambda r: xe[slot, r, group(c), :], 0, ext)
            for r in range(ext - 1):
                xq[slot, r, group(c), :] = pltpu.roll(xe[slot, r, group(c), :], last, axis=1)

        def prepare_own(c, _):
            prepare(own, c * 2)
            prepare(own, c * 2 + 1)
            return 0

        def label_rows(slot):
            for r in range(ext):
                if r < DEPTH:
                    row = lt[slot, 1, rows - DEPTH + r : rows - DEPTH + r + 1, :]
                elif r < top:
                    row = lt[slot, 0, r - DEPTH : r - DEPTH + 1, :]
                else:
                    row = lt[slot, 2, r - top : r - top + 1, :]
                lab[slot, r] = jnp.broadcast_to(row, (8, cols))
            lp[slot] = gather_edges(lambda r: lab[slot, r], 0, ext)

            def lookup(n, _):
                for r in (n * 2, n * 2 + 1):
                    parts, here = look(lab[slot, r])
                    for i in range(6):
                        coef[i, slot, r] = parts[i]
                    inside[slot, r] = here
                return 0

            lax.fori_loop(0, ext // 2, lookup, 0)

        for side in (0, 1):
            for j in range(3):
                pl.when(exists(side, j))(lambda side=side, j=j: x_copy(side, j).wait_recv())

        for c in range(lead8 // 8):
            at = slice(c * 8, c * 8 + 8)
            sides = [jnp.where(near, xr[0, j, at, :], xr[1, j, at, :]) for j in range(3)]
            corners = jnp.where(lane < 8 * DEPTH + 28, sides[2], sides[0])
            xm[own, at, :] = jnp.where(middle, sides[1], pltpu.roll(corners, 8 * rows, axis=1))

        z_start(z_rim)
        for c in range(nch // 2, nch):
            z_start(lambda i: z_copy(i, 2, c))
        y_arrive(lambda up: y_tile(noff, own, up))
        label_rows(own)
        y_arrive(lambda up: y_copy(noff, own, up, None))
        lax.fori_loop(0, groups // 2, prepare_own, 0)

        for c in range(1, nch):
            forward(c)

        for i in range(noff):
            when(z_plan(i)[4], lambda i=i: y_arrive(lambda up: y_tile(i, z_plan(i)[2], up)))
            label_rows(z_plan(i)[2])

        def ready(c):
            for i in range(noff):

                def arrived(i=i):
                    z_copy(i, 2, c).wait_recv()
                    y_arrive(lambda up: y_copy(i, z_plan(i)[2], up, c))

                when(z_plan(i)[4], arrived)

            def step(g, _):
                for i in range(noff):
                    prepare(z_plan(i)[2], c * per + g)
                return 0

            lax.fori_loop(0, per, step, 0)

        ready(0)
        for i in range(noff):
            when(z_plan(i)[4], lambda i=i: z_rim(i).wait_recv())
        for s in range(layers):
            for side in (0, 1):
                beyond = xm[s, leads:lead8, :]
                label = (
                    jnp.where(near, lp[s], beyond) if side else jnp.where(near, beyond, lp[s])
                )
                parts, here = look(label)
                for i in range(6):
                    hcoef[i, s, side] = parts[i]
                hinside[s, side] = here

        line_width = nx * cols
        column = (x * cols + lane).astype(jnp.float32)
        moved = jnp.where(lane >= cols - DEPTH, lane + DEPTH - cols, lane + DEPTH)
        packed_row = moved // 8
        packed_voxel = packed_row * line_width + (moved - packed_row * 8) + (
            x * cols + (y * rows - DEPTH) * line_width - DEPTH
        )
        ends = (lane == 0, lane == last)
        seam = (lane & 7) == 7

        def source(c, voxel):
            return jnp.where(
                elec[0, group(c), :] == voxel, 1.0,
                jnp.where(elec[1, group(c), :] == voxel, -1.0, 0.0),
            )

        def flux(t, axis, grads):
            order = ((0, 3, 4), (3, 1, 5), (4, 5, 2))[axis]
            return t[order[0]] * grads[0] + t[order[1]] * grads[1] + t[order[2]] * grads[2]

        def rim(fields, side, full):
            sums, edges = [], []
            below = None
            for s in range(layers):
                t = [hcoef[i, s, side] for i in range(6)]
                v = fields[s]
                grads = (
                    pltpu.roll(v, last, axis=1) - v,
                    pltpu.roll(v, cols - 8, axis=1) - v,
                    fields[s + 1] - v if s + 1 < layers else -v,
                )
                flux_x = flux(t, 0, grads)
                edges.append(flux_x)
                if full:
                    flux_y, flux_z = flux(t, 1, grads), flux(t, 2, grads)
                    total = (pltpu.roll(flux_y, 8, axis=1) - flux_y) + (
                        pltpu.roll(flux_x, 1, axis=1) - flux_x
                    )
                    total = total - flux_z if below is None else total + (below - flux_z)
                    below = flux_z
                    sums.append(total)
            return sums, edges

        def seams(right, edges):
            return [
                jnp.where(seam, edges[s], pltpu.roll(right[s], cols - 2, axis=1))
                for s in range(layers)
            ]

        def operate(load, emit, lo, hi, joins, count, shifted=None):
            below_y = [[None] * layers for _ in range(count)]
            if shifted is None:
                shifted = lambda k, s, r, v: pltpu.roll(v, last, axis=1)
            for r in range(lo - 1, hi):
                here = [[load(k, s, r) for s in range(layers)] for k in range(count)]
                below_z = [None] * count
                for s in range(layers):
                    t = [coef[i, s, r] for i in range(6)]
                    for k in range(count):
                        v = here[k][s]
                        join = pltpu.roll(joins[k][s], (cols + 1 - 8 * r) % cols, axis=1)
                        grads = (
                            jnp.where(ends[1], join, shifted(k, s, r, v)) - v,
                            load(k, s, r + 1) - v,
                            here[k][s + 1] - v if s + 1 < layers else -v,
                        )
                        flux_y = flux(t, 1, grads)
                        if r >= lo:
                            flux_x, flux_z = flux(t, 0, grads), flux(t, 2, grads)
                            before = jnp.where(ends[0], join, pltpu.roll(flux_x, 1, axis=1))
                            total = (below_y[k][s] - flux_y) + (before - flux_x)
                            total = total - flux_z if s == 0 else total + (below_z[k] - flux_z)
                            emit(k, s, r, total)
                            below_z[k] = flux_z
                        below_y[k][s] = flux_y

        def clip(value, s, r):
            return value if not windowed and DEPTH <= r < top else value * inside[s, r]

        plane_voxels = ny * rows * line_width

        def rims(c):
            mine = [xp[s, group(c), :] for s in range(layers)]
            beyond = [xm[s, group(c), :] for s in range(layers)]
            right = [jnp.where(near, beyond[s], mine[s]) for s in range(layers)]
            left = [jnp.where(near, mine[s], beyond[s]) for s in range(layers)]

            def keep(n, joins):
                for s in range(layers):
                    joined[n, s, group(c), :] = joins[s]

            right_sum, _ = rim(right, 0, True)
            left_sum, left_edge = rim(left, 1, True)
            keep(0, seams(right, left_edge))

            def rim_r(total, s, side):
                voxel = packed_voxel + ((first + s) * plane_voxels + (0 if side else cols))
                return (source(c, voxel.astype(jnp.float32)) - total) * hinside[s, side]

            right_r = [rim_r(right_sum[s], s, 0) for s in range(layers)]
            left_r = [rim_r(left_sum[s], s, 1) for s in range(layers)]
            right_sum, _ = rim(right_r, 0, True)
            left_sum, left_edge = rim(left_r, 1, True)
            keep(1, seams(right_r, left_edge))
            right_q = [right_sum[s] * hinside[s, 0] for s in range(layers)]
            left_q = [left_sum[s] * hinside[s, 1] for s in range(layers)]
            _, left_edge = rim(left_q, 1, False)
            keep(2, seams(right_q, left_edge))

        def joins_of(n, cs):
            return [[joined[n, s, group(c), :] for s in range(layers)] for c in cs]

        def apply_r(cs):
            def emit(k, s, r, total):
                row = (first + s) * (ny * rows) + y * rows + (r - DEPTH)
                voxel = column + (row * line_width).astype(jnp.float32)
                re[s, r, group(cs[k]), :] = clip(source(cs[k], voxel) - total, s, r)

            def load(k, s, r):
                return xe[s, r, group(cs[k]), :]

            def shifted(k, s, r, v):
                return xq[s, r, group(cs[k]), :]

            operate(load, emit, 1, ext - 1, joins_of(0, cs), len(cs), shifted)

        def apply_q(cs):
            def emit(k, s, r, total):
                qe[s, r, group(cs[k]), :] = clip(total, s, r)

            def load(k, s, r):
                return re[s, r, group(cs[k]), :]

            operate(load, emit, 2, ext - 2, joins_of(1, cs), len(cs))

        def apply_p(cs):
            def emit(k, s, r, total):
                pe[s, r - DEPTH, group(cs[k]), :] = total

            def load(k, s, r):
                return qe[s, r, group(cs[k]), :]

            operate(load, emit, 3, ext - 3, joins_of(2, cs), len(cs))
            for c in cs:
                for r in range(rows):
                    at = slice(r * cols, (r + 1) * cols)
                    base_out[group(c), at] = re[own, DEPTH + r, group(c), :]
                    base_out[group(c + groups), at] = qe[own, DEPTH + r, group(c), :]
                    base_out[group(c + 2 * groups), at] = pe[own, r, group(c), :]

        def turn(c, _):
            pl.when(c > 0)(lambda: ready(c))

            def edge(g, _):
                for k in range(TWIN):
                    rims(c * per + g * TWIN + k)
                return 0

            lax.fori_loop(0, per // TWIN, edge, 0)

            for apply, pair in ((apply_r, PAIR), (apply_q, PAIR), (apply_p, PAIR)):

                def step(g, _, apply=apply, pair=pair):
                    apply([c * per + g * pair + k for k in range(pair)])
                    return 0

                lax.fori_loop(0, per // pair, step, 0)
            return 0

        lax.fori_loop(0, nch, turn, 0)

        products = nt_dot(base_out[0 : 2 * leads, :], base_out[...])
        upper = products[0:leads, 0 : 2 * leads]
        lower = products[leads : 2 * leads, leads : 3 * leads]
        grams = jnp.concatenate([upper, lower], axis=0)
        for i in range(plane):
            gs[i] = grams[i * share : (i + 1) * share, :]

        save = pltpu.make_async_copy(base_out, base_hbm, ssem.at[0])
        save.start()

        def exchange(phase, peers, source_of, target):
            copies = [
                remote(source_of(pid), target, asend.at[phase, k], arecv.at[phase, k], device)
                for k, (pid, device) in enumerate(peers)
                if k
            ]
            for copy in copies:
                copy.start()
            for copy in copies:
                copy.wait()

        me = plane_peers[0][0]
        rs[me] = gs[me]
        exchange(0, plane_peers, lambda pid: gs.at[pid], rs.at[me])
        zs[x] = jnp.sum(rs[...], axis=0)
        exchange(1, line_peers, lambda pid: zs.at[x], zs.at[x])
        total[...] = jnp.sum(zs[...], axis=0)
        keep = pltpu.make_async_copy(total, gram_hbm.at[me], ssem.at[1])
        keep.start()
        exchange(2, plane_peers, lambda pid: total, gram_hbm.at[me])
        keep.wait()
        save.wait()

        def sent(copy):
            copy.wait_send()

        y_each(sent, lambda up: y_copy(noff, own, up, None))
        y_each(sent, lambda up: y_tile(noff, own, up))
        x_each(sent)
        for i in range(noff):
            for part in range(3):
                for c in range(nch):
                    when(z_plan(i)[3], lambda i=i, part=part, c=c: sent(z_copy(i, part, c)))
            when(z_plan(i)[3], lambda i=i: sent(z_tile(i)))
            when(z_plan(i)[3], lambda i=i: sent(z_rim(i)))

            def forwarded(i=i):
                slot = z_plan(i)[2]
                for c in range(nch):
                    y_each(sent, lambda up: y_copy(i, slot, up, c))
                y_each(sent, lambda up: y_tile(i, slot, up))

            when(z_plan(i)[4], forwarded)

    f32 = jnp.float32
    tile = (8, cols)
    group_sems = pltpu.SemaphoreType.DMA((3, max(plane, nx)))
    y_sems = pltpu.SemaphoreType.DMA((noff + 1, 2, nch + 1))
    z_sems = pltpu.SemaphoreType.DMA((noff, 3 * nch + 2))
    x_sems = pltpu.SemaphoreType.DMA((2, 3))
    call = pl.pallas_call(
        kernel,
        out_shape=(
            jax.ShapeDtypeStruct((3 * leads, rows * cols), f32),
            jax.ShapeDtypeStruct((plane, share, size), f32),
        ),
        in_specs=[pl.BlockSpec(memory_space=pltpu.HBM)] * 4,
        out_specs=[pl.BlockSpec(memory_space=pltpu.HBM)] * 2,
        scratch_shapes=[
            pltpu.VMEM((3 * leads, rows * cols), f32),
            pltpu.VMEM((share, size), f32),
            pltpu.SemaphoreType.DMA((2,)),
            pltpu.SMEM((6, classes), f32),
            pltpu.VMEM((rows, cols), jnp.int32),
            pltpu.VMEM((2, leads), jnp.int32),
            pltpu.VMEM((leads * rows, cols), f32),
            pltpu.SemaphoreType.DMA((4,)),
            pltpu.VMEM((layers, ext, leads, cols), f32),
            pltpu.VMEM((layers, 3) + tile, f32),
            pltpu.VMEM((layers, ext) + tile, f32),
            pltpu.VMEM((layers,) + tile, f32),
            pltpu.VMEM((lead8, cols), f32),
            pltpu.VMEM((2, 3, lead8, cols), f32),
            pltpu.VMEM((layers, lead8, cols), f32),
            pltpu.VMEM((layers, leads, cols), f32),
            pltpu.VMEM((layers, ext - 1, leads, cols), f32),
            pltpu.VMEM((3, layers, leads, cols), f32),
            pltpu.VMEM((layers, ext, leads, cols), f32),
            pltpu.VMEM((layers, ext, leads, cols), f32),
            pltpu.VMEM((layers, rows, leads, cols), f32),
            pltpu.VMEM((6, layers, ext) + tile, f32),
            pltpu.VMEM((layers, ext) + tile, f32),
            pltpu.VMEM((6, layers, 2) + tile, f32),
            pltpu.VMEM((layers, 2) + tile, f32),
            pltpu.VMEM((2, leads, cols), f32),
            pltpu.VMEM((plane, share, size), f32),
            pltpu.VMEM((plane, share, size), f32),
            pltpu.VMEM((nx, share, size), f32),
            z_sems, z_sems, y_sems, y_sems, x_sems, x_sems, group_sems, group_sems,
        ],
        compiler_params=pltpu.CompilerParams(
            collective_id=0, has_side_effects=True,
            vmem_limit_bytes=VMEM_LIMIT,
        ),
        name="krylov",
    )
    return call, size


def spread_row(value, row):
    return jnp.broadcast_to(value[row : row + 1, :], (8, value.shape[1]))


def solve_four(columns, row, values, sub):
    p = [[spread_row(columns[j], row + i) for j in range(4)] for i in range(4)]
    det = p[0][0] * p[1][1] - p[0][1] * p[1][0]
    e = [
        [p[1][1] * p[0][j] - p[0][1] * p[1][j] for j in (2, 3)],
        [p[0][0] * p[1][j] - p[1][0] * p[0][j] for j in (2, 3)],
    ]
    m = [
        [det * p[i][j + 2] - (p[i][0] * e[0][j] + p[i][1] * e[1][j]) for j in range(2)]
        for i in (2, 3)
    ]
    first = 1.0 / det
    second = det / (m[0][0] * m[1][1] - m[0][1] * m[1][0])
    done = []
    for value in values:
        cut = lambda v: v[:, : value.shape[1]]
        u = [spread_row(value, row + j) for j in range(4)]
        ua = (cut(p[1][1]) * u[0] - cut(p[0][1]) * u[1]) * cut(first)
        ub = (cut(p[0][0]) * u[1] - cut(p[1][0]) * u[0]) * cut(first)
        t = [u[i] - (cut(p[i][0]) * ua + cut(p[i][1]) * ub) for i in (2, 3)]
        x2 = (cut(m[1][1]) * t[0] - cut(m[0][1]) * t[1]) * cut(second)
        x3 = (cut(m[0][0]) * t[1] - cut(m[1][0]) * t[0]) * cut(second)
        x0 = ua - (cut(e[0][0]) * x2 + cut(e[0][1]) * x3) * cut(first)
        x1 = ub - (cut(e[1][0]) * x2 + cut(e[1][1]) * x3) * cut(first)
        x = (x0, x1, x2, x3)
        value = value - (
            (cut(columns[0]) * x0 + cut(columns[1]) * x1)
            + (cut(columns[2]) * x2 + cut(columns[3]) * x3)
        )
        for j in range(4):
            value = jnp.where(cut(sub) == row + j, x[j], value)
        done.append(value)
    return done


def columns_of(tile, at):
    return [jnp.broadcast_to(tile[0][:, at + j : at + j + 1], (8, 128)) for j in range(8)]


def eliminate(matrix, count):
    width = matrix.shape[1]
    cuts = [(a, min(a + 128, width)) for a in range(0, width, 128)]
    lane = lax.broadcasted_iota(jnp.int32, (8, 128), 1)
    sub = lax.broadcasted_iota(jnp.int32, (8, 128), 0)
    tiles = []
    for i in range(0, count, 8):
        parts = [matrix[i : i + 8, a:b] for a, b in cuts]
        pivot = jnp.sum(jnp.where(lane == sub + i, parts[0], 0.0), axis=1, keepdims=True)
        inverse = 1.0 / jnp.broadcast_to(pivot, (8, 128))
        tiles.append([part * inverse[:, : part.shape[1]] for part in parts])
    for home in range(count // 8):
        soon = [home + 1] if home + 1 < len(tiles) else []
        left = {i: columns_of(tiles[i], home * 8) for i in soon}
        mine = columns_of(tiles[home], home * 8)
        parts = solve_four(mine[:4], 0, mine[4:] + tiles[home], sub)
        parts = solve_four(parts[:4], 4, parts[4:], sub)
        for i in soon:
            for h, (a, b) in enumerate(cuts):
                terms = [left[i][j][:, : b - a] * spread_row(parts[h], j) for j in range(8)]
                while len(terms) > 1:
                    terms = [terms[j] + terms[j + 1] for j in range(0, len(terms), 2)]
                tiles[i][h] = tiles[i][h] - terms[0]
        rest = [i for i in range(len(tiles)) if i != home and i not in soon]
        active = jnp.concatenate([tiles[i][0][:, :count] for i in rest], axis=0)
        solved = jnp.concatenate(parts, axis=1)
        blank = lambda n: [jnp.zeros((n, width), jnp.float32)] if n else []
        padded = jnp.concatenate(
            blank(home * 8) + [solved] + blank(count - 8 - home * 8), axis=0
        )
        change = nn_dot(active, padded)
        for n, i in enumerate(rest):
            for h, (a, b) in enumerate(cuts):
                tiles[i][h] = tiles[i][h] - change[n * 8 : n * 8 + 8, a:b]
        tiles[home] = parts
    return jnp.concatenate([jnp.concatenate(tile, axis=1) for tile in tiles], axis=0)


def make_combine(leads, rows, cols):
    def kernel(
        gram_hbm, base_hbm, field_hbm, out_hbm, res_hbm, gram, base, field, out, res, isem, osem
    ):
        loads = [
            pltpu.make_async_copy(source, target, isem.at[i])
            for i, (source, target) in enumerate(
                ((gram_hbm, gram), (base_hbm, base), (field_hbm, field))
            )
        ]
        for load in loads:
            load.start()
        loads[0].wait()
        rr, rq = gram[0:leads, 0:leads], gram[0:leads, leads : 2 * leads]
        qq, qp = gram[leads : 2 * leads, 0:leads], gram[leads : 2 * leads, leads : 2 * leads]
        first = eliminate(jnp.concatenate([rq, rr, qq], axis=1), leads)
        z2, z1 = first[:, leads : 2 * leads], first[:, 2 * leads : 3 * leads]
        schur = jnp.concatenate([qp, rq], axis=1) - nn_dot(qq, jnp.concatenate([z1, z2], axis=1))
        e = eliminate(schur, leads)[:, leads : 2 * leads]
        c = z2 - nn_dot(z1, e)
        mix = jnp.transpose(jnp.concatenate([c, e], axis=0))
        for load in loads[1:]:
            load.wait()
        gain = nn_dot(mix, base[0 : 2 * leads, :])
        for r in range(rows):
            at = slice(r * cols, (r + 1) * cols)
            spread = pl.ds(r, leads, stride=rows)
            out[spread, :] = field[spread, :] + gain[:, at]
        saves = [
            pltpu.make_async_copy(source, target, osem.at[i])
            for i, (source, target) in enumerate(((out, out_hbm), (res, res_hbm)))
        ]
        saves[0].start()
        loss = nn_dot(mix, base[leads : 3 * leads, :])
        for r in range(rows):
            at = slice(r * cols, (r + 1) * cols)
            res[pl.ds(r, leads, stride=rows), :] = base[0:leads, at] - loss[:, at]
        saves[1].start()
        for save in saves:
            save.wait()

    f32 = jnp.float32
    hbm = pl.BlockSpec(memory_space=pltpu.HBM)
    shape = jax.ShapeDtypeStruct((leads * rows, cols), f32)
    block = pltpu.VMEM((leads * rows, cols), f32)
    return pl.pallas_call(
        kernel,
        out_shape=(shape, shape),
        in_specs=[hbm] * 3,
        out_specs=(hbm, hbm),
        scratch_shapes=[
            pltpu.VMEM((2 * leads, 2 * leads), f32),
            pltpu.VMEM((3 * leads, rows * cols), f32),
            block, block, block,
            pltpu.SemaphoreType.DMA((3,)),
            pltpu.SemaphoreType.DMA((2,)),
        ],
        compiler_params=pltpu.CompilerParams(vmem_limit_bytes=VMEM_LIMIT),
        name="combine",
    )


def solution(mesh):
    nz, ny, nx = (mesh.shape[name] for name in ("gz", "gy", "gx"))

    def body(labels, tissue_tensors, electrodes, initial):
        leads, _, rows, cols = initial.shape
        field = initial.reshape(leads * rows, cols)
        krylov, size = make_krylov(
            nz, ny, nx, leads, rows, cols, tissue_tensors.shape[1]
        )
        base, gram = krylov(tissue_tensors, labels.reshape(rows, cols), electrodes, field)
        out, res = make_combine(leads, rows, cols)(gram.reshape(size, size), base, field)
        return out.reshape(initial.shape), res.reshape(initial.shape)

    placed = (P("gz", "gy", "gx"), P(), P(), P(None, "gz", "gy", "gx"))
    return jax.shard_map(
        body,
        mesh=mesh,
        in_specs=placed,
        out_specs=(P(None, "gz", "gy", "gx"), P(None, "gz", "gy", "gx")),
        check_vma=False,
    )
```
